128 devices in a mesh: grp: 8 (over z, core), ch: 16 (over y, x).
Axes of the slice: x: 4, y: 4, z: 4, core: 2. Of those that a mesh axis runs over, the one named last changes fastest.
Arguments:
- features: bfloat16 [256, 64, 512], P(('grp', 'ch')), may hold values from -6 to 6
- live_counts: int32 [128], P(('grp', 'ch')), may hold values from 1 to 2, as said below
- neighbours: int32 [256, 27], P(('grp', 'ch')), may hold values from -1 to 255, as said below
- w_first: bfloat16 [27, 64, 64], replicated, may hold values from -0.21875 to 0.21875
- w_second: bfloat16 [27, 64, 64], replicated, may hold values from -0.21875 to 0.21875
- w_middle: bfloat16 [27, 128, 64], replicated, may hold values from -0.3125 to 0.3125
- w_coarse: bfloat16 [27, 256, 128], P(None, 'ch'), may hold values from -0.21875 to 0.21875
- w_project: bfloat16 [256, 64], P('ch'), may hold values from -0.75 to 0.75
- w_output: bfloat16 [64, 128], replicated, may hold values from -0.5 to 0.5
Outputs:
- mixed_out: bfloat16 [256, 64, 512], P(('grp', 'ch'))
The draws below stay inside these ranges and needn't reach their ends.
Inputs may be any that keep to these rules, and one draw needn't show every extreme that they name: Device d holds its live blocks in slots d * 2 to d * 2 + live_counts[d] - 1; the rest are padding. In every group of devices along ch one device holds exactly 2. `neighbours`: the live blocks occupy distinct positions of a lattice of 16 x 16 x (2 times the size of grp) positions; the devices with grp index g hold exactly the blocks of layers g * 2 to (g + 1) * 2 - 1 along z. Within a group, the device with ch index m (of n) holds blocks only in the tile of x from floor(2 m / n) * 8 to that plus 16 / 2 - 1 and y from (m mod (n / 2)) * 2 * 16 / n to that plus 2 * 16 / n - 1. For a live block b, entry 9 (dx + 1) + 3 (dy + 1) + dz + 1 is the block at b's position plus (dx, dy, dz), or -1 where that position is empty or off the lattice; entry 13 is b itself. Rows of padding slots are all -1, and no entry names a padding slot.
All inputs are finite; a program needn't handle non-finite values.
Results may differ from the reference program's by a relative error of at most 0.013.
Values may be sent and summed in bfloat16 or wider, within the bound.
No kernel may reach another device: no remote copies, remote signals or barrier semaphores. Data moves between devices by JAX's collectives and lax.ppermute only.
A program may use at most 128 MiB of HBM per device.

```python
import jax
import jax.numpy as jnp
from jax import lax

C0 = 64
C1 = 128
C2 = 256
EDGE = 8
SIDE = 16
LAYERS = 2
BLK_DEV = 2
GROUP_BLOCKS = 32
BLOCKS = 256


def scene(key):
    base_key = jax.random.fold_in(key, 11)
    counts_key, choose_key, order_key = jax.random.split(base_key, 3)
    groups = BLOCKS // GROUP_BLOCKS
    members = GROUP_BLOCKS // BLK_DEV
    places = SIDE * SIDE * LAYERS
    tile_size = places // members
    half_members = members // 2
    tile_x = SIDE // 2
    tile_y = SIDE // half_members
    lowest = max(BLK_DEV // 2, 1)
    counts = jax.random.randint(counts_key, (groups, members), lowest, BLK_DEV + 1)
    fullest = jax.random.randint(choose_key, (groups, 1), 0, members)
    counts = jnp.where(jnp.arange(members)[None, :] == fullest, BLK_DEV, counts).astype(jnp.int32)
    member_keys = jax.random.split(order_key, groups * members)
    orders = jax.vmap(lambda one_key: jax.random.permutation(one_key, tile_size))(member_keys)
    local = orders.reshape(groups, members, tile_size)[:, :, :BLK_DEV].astype(jnp.int32)
    slot_index = jnp.arange(BLK_DEV, dtype=jnp.int32)[None, None, :]
    member_ids = jnp.arange(members, dtype=jnp.int32)[None, :, None]
    group_ids = jnp.arange(groups, dtype=jnp.int32)[:, None, None]
    living = slot_index < counts[:, :, None]
    coord_x = member_ids // half_members * tile_x + local // (tile_y * LAYERS)
    coord_y = member_ids % half_members * tile_y + local // LAYERS % tile_y
    coord_z = local % LAYERS + group_ids * LAYERS
    place_all = coord_z // LAYERS * places + coord_x * SIDE * LAYERS + coord_y * LAYERS + coord_z % LAYERS
    ids = group_ids * GROUP_BLOCKS + member_ids * BLK_DEV + slot_index
    target = jnp.where(living, place_all, groups * places).reshape(-1)
    block_id = jnp.full((groups * places,), -1, jnp.int32).at[target].set(ids.reshape(-1).astype(jnp.int32), mode='drop')
    columns = []
    for shift_x in (-1, 0, 1):
        for shift_y in (-1, 0, 1):
            for shift_z in (-1, 0, 1):
                next_x = coord_x + shift_x
                next_y = coord_y + shift_y
                next_z = coord_z + shift_z
                inside = (next_x >= 0) & (next_x < SIDE) & (next_y >= 0) & (next_y < SIDE) & (next_z >= 0) & (next_z < groups * LAYERS)
                place = next_z // LAYERS * places + next_x * SIDE * LAYERS + next_y * LAYERS + next_z % LAYERS
                found = jnp.take(block_id, jnp.clip(place, 0, groups * places - 1))
                columns.append(jnp.where(inside & living, found, -1))
    table = jnp.stack(columns, axis=-1).reshape(BLOCKS, 27).astype(jnp.int32)
    return (counts.reshape(-1), table)


def draw_live_counts(key, part):
    return scene(key)[0]


def draw_neighbours(key, part):
    return scene(key)[1]


def steps_of(own_key, shape, pieces, low, high):
    loudness = 1.0
    for axis_at, blocks in pieces:
        heights = jax.random.uniform(jax.random.fold_in(jax.random.fold_in(own_key, 6), axis_at), (blocks,), jnp.float32, low / len(pieces), high / len(pieces))
        loudness = loudness * jnp.repeat(jnp.exp(heights), shape[axis_at] // blocks).reshape((-1,) + (1,) * (len(shape) - 1 - axis_at))
    return loudness


def normal_values(stream_key, extent, width, reach, cuts=(), kind=jnp.bfloat16):
    level = steps_of(stream_key, extent, cuts, -0.22, 0.18) if cuts else 1.0
    values = jax.random.normal(stream_key, extent, jnp.float32) * width * level
    return jnp.minimum(jnp.maximum(values, -reach), reach).astype(kind)


def setup_inputs(seed: int = 0) -> dict:
    splits = jax.random.split(jax.random.key(seed), 10)
    features = normal_values(splits[0], (BLOCKS, C0, EDGE ** 3), 1.0, 6.0, ((0, 128),))
    live_counts = draw_live_counts(jax.random.fold_in(splits[9], 71), 0)
    neighbours = draw_neighbours(jax.random.fold_in(splits[9], 71), 0)
    w_first = normal_values(splits[3], (27, C0, C0), (27 * C0 // 2) ** -0.5, 0.21875)
    w_second = normal_values(splits[4], (27, C0, C0), (27 * C0 // 2) ** -0.5, 0.21875)
    w_middle = normal_values(splits[5], (27, C1, C0), (27 * C0 // 4) ** -0.5, 0.3125)
    w_coarse = normal_values(splits[6], (27, C2, C1), (27 * C1 // 4) ** -0.5, 0.21875, ((1, 16),))
    w_project = normal_values(splits[7], (C2, C0), (C2 // 4) ** -0.5, 0.75, ((0, 16),))
    w_output = normal_values(splits[8], (C0, 2 * C0), (2 * C0) ** -0.5, 0.5)
    return dict(features=features, live_counts=live_counts, neighbours=neighbours, w_first=w_first, w_second=w_second, w_middle=w_middle, w_coarse=w_coarse, w_project=w_project, w_output=w_output)


offsets = [(shift_x, shift_y, shift_z) for shift_x in (-1, 0, 1) for shift_y in (-1, 0, 1) for shift_z in (-1, 0, 1)]


def ranges_for(step_in, margin, length):
    if step_in < 0:
        return 0, margin, length - margin, length
    if step_in == 0:
        return margin, margin + length, 0, length
    return margin + length, length + 2 * margin, 0, margin


def extend(volume, neighbour_rows, margin):
    count_rows = neighbour_rows.shape[0]
    channels = volume.shape[1]
    length = volume.shape[2]
    side_out = length + 2 * margin
    result = jnp.zeros((count_rows, channels, side_out, side_out, side_out), jnp.float32)
    for column, (shift_x, shift_y, shift_z) in enumerate(offsets):
        target = neighbour_rows[:, column]
        safe_rows = jnp.clip(target, 0, volume.shape[0] - 1)
        low_x, high_x, from_x, till_x = ranges_for(shift_x, margin, length)
        low_y, high_y, from_y, till_y = ranges_for(shift_y, margin, length)
        low_z, high_z, from_z, till_z = ranges_for(shift_z, margin, length)
        portion = volume[safe_rows, :, from_x:till_x, from_y:till_y, from_z:till_z]
        portion = jnp.where((target >= 0)[:, None, None, None, None], portion, jnp.zeros_like(portion))
        result = result.at[:, :, low_x:high_x, low_y:high_y, low_z:high_z].set(portion)
    return result


def convolve(padded, weight):
    inside = padded.shape[2] - 2
    summed = None
    for column, (shift_x, shift_y, shift_z) in enumerate(offsets):
        window = padded[:, :, 1 + shift_x:1 + shift_x + inside, 1 + shift_y:1 + shift_y + inside, 1 + shift_z:1 + shift_z + inside]
        product_term = jnp.einsum("oc,bcxyz->boxyz", weight[column].astype(jnp.float32), window, precision=lax.Precision.HIGHEST)
        summed = product_term if summed is None else summed + product_term
    return summed


def layer(volume, neighbours, weight, batches):
    grouped = neighbours.reshape(batches, -1, 27)

    def one_batch(neighbour_rows):
        return jax.nn.gelu(convolve(extend(volume, neighbour_rows, 1), weight)).astype(jnp.bfloat16)

    output = lax.map(one_batch, grouped)
    return output.reshape((volume.shape[0],) + output.shape[2:])


def pooled(volume):
    count_rows, channels, length = volume.shape[0], volume.shape[1], volume.shape[2]
    halved = length // 2
    blocked = volume.astype(jnp.float32).reshape(count_rows, channels, halved, 2, halved, 2, halved, 2)
    return (jnp.sum(blocked, axis=(3, 5, 7)) * 0.125).astype(jnp.bfloat16)


def reference(features, live_counts, neighbours, w_first, w_second, w_middle, w_coarse, w_project, w_output):
    batches = BLOCKS // GROUP_BLOCKS
    volume = features.reshape(BLOCKS, C0, EDGE, EDGE, EDGE).astype(jnp.float32)
    first_out = layer(volume, neighbours, w_first, batches)
    second = layer(first_out.astype(jnp.float32), neighbours, w_second, batches)
    middle_in = pooled(second)
    middle = layer(middle_in.astype(jnp.float32), neighbours, w_middle, batches)
    coarse_in = pooled(middle)
    hidden = layer(coarse_in.astype(jnp.float32), neighbours, w_coarse, batches)
    coarse = jnp.einsum("ko,bkxyz->boxyz", w_project.astype(jnp.float32), hidden.astype(jnp.float32), precision=lax.Precision.HIGHEST).astype(jnp.bfloat16)
    factor = EDGE // coarse.shape[2]
    widened = jnp.repeat(jnp.repeat(jnp.repeat(coarse, factor, axis=2), factor, axis=3), factor, axis=4)
    skipped = jnp.einsum("oc,bcxyz->boxyz", w_output[:, :C0].astype(jnp.float32), second.astype(jnp.float32), precision=lax.Precision.HIGHEST)
    lifted = jnp.einsum("oc,bcxyz->boxyz", w_output[:, C0:].astype(jnp.float32), widened.astype(jnp.float32), precision=lax.Precision.HIGHEST)
    mixed_out = skipped + lifted
    slot_ids = jnp.arange(BLOCKS, dtype=jnp.int32)
    living = (slot_ids % BLK_DEV) < live_counts[slot_ids // BLK_DEV]
    mixed_out = jnp.where(living[:, None, None, None, None], mixed_out, jnp.zeros_like(mixed_out))
    return mixed_out.astype(jnp.bfloat16).reshape(BLOCKS, C0, EDGE ** 3)
```

```python
import functools

import jax
import jax.numpy as jnp
import numpy as np
from jax import lax
from jax.experimental import pallas as pl
from jax.experimental.pallas import tpu as pltpu
from jax.sharding import PartitionSpec as P

AXES = ("grp", "ch")
BF = jnp.bfloat16
F32 = jnp.float32
VMEM = pl.BlockSpec(memory_space=pltpu.VMEM)
SMEM = pl.BlockSpec(memory_space=pltpu.SMEM)
ANY = pl.BlockSpec(memory_space=pl.ANY)
PARAMS = pltpu.CompilerParams(vmem_limit_bytes=48 * 2**20)

ATOM = (2, 16, 128)
ABSENT = 96


def tables():
    step = (-1, 0, 0, 1)
    half = (1, 0, 1, 0)
    atoms = np.zeros((4, 128, 54), np.int32)
    for b in range(2):
        for z in range(4):
            for x in range(4):
                for y in range(4):
                    a = ((b * 4 + z) * 4 + x) * 4 + y
                    n = b * 27 + 9 * (step[x] + 1) + 3 * (step[y] + 1) + step[z] + 1
                    atoms[:, a, n] = (1, half[z], half[y], half[x])
    taps = np.zeros((432, 54), np.int32)
    inner = np.zeros((432, 1), np.int32)
    for t in range(27):
        tx, ty, tz = t // 9, t // 3 % 3, t % 3
        for r in range(16):
            y, b, z, x = r // 8, r // 4 % 2, r // 2 % 2, r % 2
            pz, px, py = z + tz, x + tx, y + ty
            n = b * 27 + 9 * (step[px] + 1) + 3 * (step[py] + 1) + step[pz] + 1
            taps[t * 16 + r, n] = 1
            inner[t * 16 + r] = half[py] * 8 + half[pz] * 2 + half[px]
    return atoms, taps, inner


def pairs_for(step_h, step_j, step_g, sizes):
    groups, members = sizes
    tiles = members // 2
    found = []
    for g in range(groups):
        for m in range(members):
            h, j = m // tiles, m % tiles
            if 0 <= j + step_j < tiles and 0 <= g + step_g < groups:
                to = (1 - h if step_h else h) * tiles + j + step_j
                found.append((g * members + m, (g + step_g) * members + to))
    return found


def gelu(v):
    return jax.nn.gelu(v, approximate=True)


def halves(axis_size_lanes):
    return lax.broadcasted_iota(jnp.int32, (1, axis_size_lanes), 1) < 64


def dot(a, b):
    return jnp.dot(a, b, preferred_element_type=F32)


def pack_kernel(half_ref, features_ref, atoms_ref, send_ref, turned):
    h = half_ref[0]
    turned[...] = features_ref[...].astype(F32).reshape(128, 512).T
    low = halves(128)
    upper = lax.broadcasted_iota(jnp.int32, (1, 8, 1), 1) < 4
    for pair in range(4):
        even = turned[pl.ds(2 * pair, 64, stride=8), :]
        odd = turned[pl.ds(2 * pair + 1, 64, stride=8), :]
        first = jnp.where(low, even, pltpu.roll(odd, 64, 1))
        second = jnp.where(low, pltpu.roll(even, 64, 1), odd)
        for b, rows in enumerate((first, second)):
            rows = rows.reshape(4, 2, 8, 128)
            a, c = rows[:, 0], rows[:, 1]
            near = jnp.where(upper, a, pltpu.roll(c, 4, 1))
            far = jnp.where(upper, pltpu.roll(a, 4, 1), c)
            for yh, part in enumerate((near, far)):
                part = part.reshape(2, 16, 128).astype(BF)
                for xh in range(2):
                    atoms_ref[pair // 2, yh, xh, b, pair % 2] = part[xh]
                send_ref[pair // 2, yh, b, pair % 2] = jnp.where(h == 0, part[1], part[0])


def widen_kernel(weight_ref, out_ref, *, outs):
    zero = jnp.zeros((outs, 64), F32)
    for tx in range(3):
        for ty in range(3):
            w = [weight_ref[9 * tx + 3 * ty + tz].astype(F32) for tz in range(3)]
            for pair, blocks in enumerate(
                (((w[0], w[1]), (zero, w[0])), ((w[2], zero), (w[1], w[2])))
            ):
                wide = jnp.concatenate([jnp.concatenate(two, axis=1) for two in blocks], axis=0)
                row = tx * 256 + pair * 128
                out_ref[row : row + 128, ty * 2 * outs : (ty + 1) * 2 * outs] = wide.T.astype(BF)


def leaf_conv(source, b, k, length, weight_ref):
    parts = [
        source[b, k + dk, dx : dx + length].reshape(length * 16, 128)
        for dx in range(3)
        for dk in range(2)
    ]
    wide = dot(jnp.concatenate(parts, axis=1), weight_ref[...])
    return (
        wide[:, 128:256]
        + pltpu.roll(wide[:, :128], 1, 0)
        + pltpu.roll(wide[:, 256:], length * 16 - 1, 0)
    )


def main_kernel(
    atom_ref, present_ref, own, below_y, above_y, below_z, above_z, w1, w2, w3,
    skip_ref, coarse_ref,
    table, wide, first, second, masks, rows_a, middle_in, rows_b, turned, sems,
):
    copies = [
        pltpu.make_async_copy(
            own.at[zh, yh], table.at[pl.ds((zh * 4 + yh) * 6, 6)], sems.at[zh * 2 + yh]
        )
        for zh in range(2)
        for yh in range(2)
    ]
    for n, source in enumerate((below_y, above_y)):
        copies += [
            pltpu.make_async_copy(
                source.at[zh], table.at[pl.ds((zh * 4 + 2 + n) * 6, 6)], sems.at[4 + n * 2 + zh]
            )
            for zh in range(2)
        ]
    for n, source in enumerate((below_z, above_z)):
        copies.append(
            pltpu.make_async_copy(source, table.at[pl.ds(48 + n * 24, 24)], sems.at[8 + n])
        )
    for copy in copies:
        copy.start()
    table[ABSENT] = jnp.zeros(ATOM, BF)

    low = halves(128)
    y_row = lax.broadcasted_iota(jnp.int32, (16, 128), 0)
    for b in range(2):
        for dx in range(3):
            of_z = []
            for dz in range(3):
                p = [
                    present_ref[b * 27 + 9 * dx + 3 * dy + dz].astype(F32) for dy in range(3)
                ]
                of_z.append(jnp.where(y_row < 4, p[0], jnp.where(y_row < 12, p[1], p[2])))
            masks[b, 0, dx] = of_z[0]
            masks[b, 1, dx] = jnp.where(low, of_z[0], of_z[1])
            masks[b, 2, dx] = of_z[1]
            masks[b, 3, dx] = jnp.where(low, of_z[1], of_z[2])
            masks[b, 4, dx] = of_z[2]

    for copy in copies:
        copy.wait()

    upper = lax.broadcasted_iota(jnp.int32, (1, 1, 8, 1), 2) < 4
    for b in range(2):
        for z in range(4):
            for x in range(4):
                base = ((b * 4 + z) * 4 + x) * 4
                a = [
                    table[atom_ref[base + y]].astype(F32).reshape(2, 2, 8, 128) for y in range(4)
                ]
                r = [pltpu.roll(v.reshape(4, 8, 128), 4, 1).reshape(2, 2, 8, 128) for v in a]
                even = jnp.concatenate(
                    [jnp.where(upper, a[0], r[1]), jnp.where(upper, a[2], r[3])], axis=2
                ).astype(BF)
                odd = jnp.concatenate(
                    [jnp.where(upper, r[0], a[1]), jnp.where(upper, r[2], a[3])], axis=2
                ).astype(BF)
                for pair in range(2):
                    for k in range(2):
                        wide[b, 2 * z + pair, 4 * x + 2 * k] = even[pair, k]
                        wide[b, 2 * z + pair, 4 * x + 2 * k + 1] = odd[pair, k]

    def masked(value, b, pattern, edge):
        mask = [masks[b, pattern, dx][None] for dx in range(3)]
        value = value.reshape(8 + 2 * edge, 16, 128)
        return jnp.concatenate(
            [value[:edge] * mask[0], value[edge : edge + 8] * mask[1], value[edge + 8 :] * mask[2]],
            axis=0,
        )

    for b in range(2):

        def first_step(k, _, b=b):
            value = gelu(leaf_conv(wide, b, k, 14, w1))
            pattern = jnp.minimum(k, 2) + jnp.maximum(k - 4, 0)
            first[b, k] = masked(value, b, pattern, 3).astype(BF)
            return 0

        lax.fori_loop(0, 7, first_step, 0)

    for b in range(2):

        def second_step(k, _, b=b):
            value = gelu(leaf_conv(first, b, k, 12, w2))
            pattern = 2 * (jnp.minimum(k, 1) + jnp.maximum(k - 4, 0))
            second[b, k] = masked(value, b, pattern, 2).astype(BF)
            return 0

        lax.fori_loop(0, 6, second_step, 0)

    for b in range(2):
        layers = []
        for k in range(6):
            v = second[b, k].astype(F32)
            v = (v.reshape(6, 2, 16, 128)[:, 0] + v.reshape(6, 2, 16, 128)[:, 1]).reshape(96, 128)
            v = v + pltpu.roll(v, 64, 1)
            rows_a[b, k] = v + pltpu.roll(v, 95, 0)
            layers.append((rows_a[b, k, pl.ds(0, 48, stride=2), :] * 0.125).astype(BF).astype(F32))
        for pair in range(3):
            middle_in[b, pair] = jnp.where(low, layers[2 * pair], layers[2 * pair + 1])

    operands = []
    for b in range(2):
        for k in range(2):
            operands.append(
                jnp.concatenate(
                    [
                        middle_in[b, k + dk, dx * 8 : dx * 8 + 32]
                        for dx in range(3)
                        for dk in range(2)
                    ],
                    axis=1,
                )
            )
    deep = dot(jnp.concatenate(operands, axis=0).astype(BF), w3[...])
    deep = (
        deep[:, 256:512] + pltpu.roll(deep[:, :256], 1, 0) + pltpu.roll(deep[:, 512:], 127, 0)
    )
    deep = gelu(deep).astype(BF).astype(F32)
    deep = (deep[:, :128] + deep[:, 128:]).reshape(8, 2, 8, 128)
    deep = (deep[:, 0] + deep[:, 1]).reshape(64, 128)
    rows_b[...] = deep + pltpu.roll(deep, 63, 0)
    coarse_ref[...] = (
        jnp.concatenate(
            [rows_b[pl.ds(2, 8, stride=8), :], rows_b[pl.ds(4, 8, stride=8), :]], axis=0
        )
        * 0.125
    ).astype(BF)

    for pair in range(4):
        v = [
            second[b, 1 + pair, 2:10].astype(F32)[:, 4:12, :].reshape(64, 128) for b in range(2)
        ]
        turned[pl.ds(2 * pair, 64, stride=8), :] = jnp.where(low, v[0], pltpu.roll(v[1], 64, 1))
        turned[pl.ds(2 * pair + 1, 64, stride=8), :] = jnp.where(
            low, pltpu.roll(v[0], 64, 1), v[1]
        )
    skip_ref[...] = turned[...].T.astype(BF).reshape(2, 64, 512)


def last_kernel(live_ref, tap_ref, own, below, above, weights, w_output, skip_ref, out_ref):
    tiles = jnp.concatenate([r[...].reshape(96, 128) for r in (own, below, above)], axis=0)
    chosen = (tap_ref[...] == lax.broadcasted_iota(jnp.int32, (432, 288), 1)).astype(F32).astype(BF)
    taps = dot(chosen, tiles).astype(BF)
    total = jnp.zeros((16, 256), F32)
    for t in range(27):
        total = total + lax.dot_general(
            taps[t * 16 : (t + 1) * 16],
            weights[:, t].reshape(256, 128),
            (((1,), (1,)), ((), ())),
            preferred_element_type=F32,
        )
    hidden = gelu(total).astype(BF)
    coarse = dot(hidden, weights[:, 27].reshape(256, 128)).astype(BF).astype(F32)
    coarse = coarse.T[:64].astype(BF)
    row = lax.broadcasted_iota(jnp.int32, (16, 512), 0)
    voxel = lax.broadcasted_iota(jnp.int32, (16, 512), 1)
    place = ((voxel >> 5) & 1) * 8 + ((voxel >> 2) & 1) * 2 + ((voxel >> 8) & 1)
    for b in range(2):
        spread = (row == place + b * 4).astype(F32).astype(BF)
        widened = dot(coarse, spread).astype(BF)
        mixed = dot(w_output[...], jnp.concatenate([skip_ref[b], widened], axis=0))
        mixed = jnp.where(b < live_ref[0], mixed, 0.0)
        out_ref[b] = mixed.astype(BF)


def shape(dims, kind=BF):
    return jax.ShapeDtypeStruct(dims, kind)


def widened_weight(weight, outs):
    return pl.pallas_call(
        functools.partial(widen_kernel, outs=outs),
        out_shape=shape((768, 6 * outs)),
        in_specs=[VMEM],
        out_specs=VMEM,
        compiler_params=PARAMS,
    )(weight)


def shards(
    features, live_counts, neighbours, w_first, w_second, w_middle, w_coarse, w_project, w_output
):
    sizes = (lax.axis_size("grp"), lax.axis_size("ch"))
    g, m = lax.axis_index("grp"), lax.axis_index("ch")
    h, j = m // 8, m % 8

    def moved(value, step_h, step_j, step_g):
        return lax.ppermute(value, AXES, pairs_for(step_h, step_j, step_g, sizes))

    shard = jnp.concatenate(
        [w_coarse, jnp.pad(w_project, ((0, 0), (0, 64)))[None]], axis=0
    )
    weights = lax.all_gather(shard, "ch", axis=0)

    atoms, send = pl.pallas_call(
        pack_kernel,
        out_shape=(shape((2, 2, 2, 2) + ATOM), shape((2, 2, 2) + ATOM)),
        in_specs=[SMEM, VMEM],
        out_specs=(VMEM, VMEM),
        scratch_shapes=[pltpu.VMEM((512, 128), F32)],
        compiler_params=PARAMS,
    )(h[None].astype(jnp.int32), features)
    beside = moved(send, 1, 0, 0)
    own = jnp.concatenate([atoms, beside[:, :, None]], axis=2)
    below_y = moved(own[:, 1], 0, 1, 0)
    above_y = moved(own[:, 0], 0, -1, 0)
    whole = [jnp.concatenate([own[z], below_y[z][None], above_y[z][None]], axis=0) for z in (0, 1)]
    below_z = moved(whole[1], 0, 0, 1)
    above_z = moved(whole[0], 0, 0, -1)

    atom_table, tap_table, inner = tables()
    entry = neighbours.reshape(54)
    present = entry >= 0
    group = entry // 32 - g
    member = entry % 32 // 2
    slot = entry % 2
    other = member // 8 != h
    tile = member % 8 - j
    base = (
        jnp.where(group == 0, 0, jnp.where(group < 0, 48, 72))
        + jnp.where(tile == 0, 0, jnp.where(tile < 0, 12, 18))
        + jnp.where(other, 4, 0)
        + slot
    )
    kept = jnp.stack(
        [
            jnp.where(present, base, ABSENT),
            jnp.where(present & (group == 0), 24, 0),
            jnp.where(present & (tile == 0), 6, 0),
            jnp.where(present & ~other, 2, 0),
        ]
    )
    atom_rows = jnp.sum(jnp.asarray(atom_table) * kept[:, None, :], axis=(0, 2))
    code = (
        jnp.where(group == 0, 0, jnp.where(group < 0, 6, 12))
        + jnp.where(tile == 0, 0, jnp.where(tile < 0, 2, 4))
        + jnp.where(other, 1, 0)
    ) * 16 + slot * 4
    code = jnp.where(present, code, -4096)
    tap_rows = jnp.sum(jnp.asarray(tap_table) * code[None], axis=1, keepdims=True) + inner

    w1 = widened_weight(w_first, 64)
    w2 = widened_weight(w_second, 64)
    w3 = widened_weight(w_middle, 128)
    skip, coarse = pl.pallas_call(
        main_kernel,
        out_shape=(shape((2, 64, 512)), shape((16, 128))),
        in_specs=[SMEM] * 2 + [ANY] * 5 + [VMEM] * 3,
        out_specs=(VMEM, VMEM),
        scratch_shapes=[
            pltpu.VMEM((97,) + ATOM, BF),
            pltpu.VMEM((2, 8, 16, 16, 128), BF),
            pltpu.VMEM((2, 7, 14, 16, 128), BF),
            pltpu.VMEM((2, 6, 12, 16, 128), BF),
            pltpu.VMEM((2, 5, 3, 16, 128), F32),
            pltpu.VMEM((2, 6, 96, 128), F32),
            pltpu.VMEM((2, 3, 48, 128), F32),
            pltpu.VMEM((64, 128), F32),
            pltpu.VMEM((512, 128), F32),
            pltpu.SemaphoreType.DMA((10,)),
        ],
        compiler_params=PARAMS,
    )(
        atom_rows,
        present.astype(jnp.int32),
        own.reshape((2, 2, 6) + ATOM),
        below_y.reshape((2, 6) + ATOM),
        above_y.reshape((2, 6) + ATOM),
        below_z.reshape((24,) + ATOM),
        above_z.reshape((24,) + ATOM),
        w1,
        w2,
        w3,
    )

    both = jnp.stack([coarse, moved(coarse, 1, 0, 0)])
    layer = jnp.concatenate([both, moved(both, 0, 1, 0), moved(both, 0, -1, 0)], axis=0)
    below, above = moved(layer, 0, 0, 1), moved(layer, 0, 0, -1)
    return pl.pallas_call(
        last_kernel,
        out_shape=shape((2, 64, 512)),
        in_specs=[SMEM] + [VMEM] * 7,
        out_specs=VMEM,
        compiler_params=PARAMS,
    )(live_counts, tap_rows, layer, below, above, weights, w_output, skip)


def solution(mesh):
    return jax.shard_map(
        shards,
        mesh=mesh,
        in_specs=(
            P(AXES, None, None),
            P(AXES),
            P(AXES, None),
            P(),
            P(),
            P(),
            P(None, "ch", None),
            P("ch", None),
            P(),
        ),
        out_specs=P(AXES, None, None),
        check_vma=False,
    )
```

```python
import functools

import jax
import jax.numpy as jnp
import numpy as np
from jax import lax
from jax.experimental import pallas as pl
from jax.experimental.pallas import tpu as pltpu
from jax.sharding import PartitionSpec as P

AXES = ("grp", "ch")
BF = jnp.bfloat16
F32 = jnp.float32
VMEM = pl.BlockSpec(memory_space=pltpu.VMEM)
SMEM = pl.BlockSpec(memory_space=pltpu.SMEM)
ANY = pl.BlockSpec(memory_space=pl.ANY)
PARAMS = pltpu.CompilerParams(vmem_limit_bytes=48 * 2**20)

ATOM = (2, 16, 128)
ABSENT = 96


def tables():
    step = (-1, 0, 0, 1)
    half = (1, 0, 1, 0)
    atoms = np.zeros((4, 128, 54), np.int32)
    for b in range(2):
        for z in range(4):
            for x in range(4):
                for y in range(4):
                    a = ((b * 4 + z) * 4 + x) * 4 + y
                    n = b * 27 + 9 * (step[x] + 1) + 3 * (step[y] + 1) + step[z] + 1
                    atoms[:, a, n] = (1, half[z], half[y], half[x])
    taps = np.zeros((432, 54), np.int32)
    inner = np.zeros((432, 1), np.int32)
    for t in range(27):
        tx, ty, tz = t // 9, t // 3 % 3, t % 3
        for r in range(16):
            y, b, z, x = r // 8, r // 4 % 2, r // 2 % 2, r % 2
            pz, px, py = z + tz, x + tx, y + ty
            n = b * 27 + 9 * (step[px] + 1) + 3 * (step[py] + 1) + step[pz] + 1
            taps[t * 16 + r, n] = 1
            inner[t * 16 + r] = half[py] * 8 + half[pz] * 2 + half[px]
    return atoms, taps, inner


def pairs_for(step_h, step_j, step_g, sizes):
    groups, members = sizes
    tiles = members // 2
    found = []
    for g in range(groups):
        for m in range(members):
            h, j = m // tiles, m % tiles
            to = (1 - h if step_h else h) * tiles + (j + step_j) % tiles
            found.append((g * members + m, (g + step_g) % groups * members + to))
    return found


def swapped(value, axis_mask, group_mask, sizes):
    groups, members = sizes
    pairs = [
        (g * members + m, (g ^ group_mask) * members + (m ^ axis_mask))
        for g in range(groups)
        for m in range(members)
    ]
    return lax.ppermute(value, AXES, pairs)


def gelu(v):
    return jax.nn.gelu(v, approximate=True)


def halves(axis_size_lanes):
    return lax.broadcasted_iota(jnp.int32, (1, axis_size_lanes), 1) < 64


def dot(a, b):
    return jnp.dot(a, b, preferred_element_type=F32)


def pack_kernel(
    place_ref, features_ref, w_coarse_ref, w_project_ref, atoms_ref, send_ref, share_ref, turned
):
    h, core = place_ref[0], place_ref[1]

    @pl.when(core == 0)
    def _():
        share_ref[...] = w_coarse_ref[0:14]

    @pl.when(core == 1)
    def _():
        share_ref[0:13] = w_coarse_ref[14:27]
        project = w_project_ref[...].astype(F32)
        share_ref[13] = jnp.concatenate([project, jnp.zeros_like(project)], axis=1).astype(BF)

    turned[...] = features_ref[...].astype(F32).reshape(128, 512).T
    low = halves(128)
    upper = lax.broadcasted_iota(jnp.int32, (1, 8, 1), 1) < 4
    for pair in range(4):
        even = turned[pl.ds(2 * pair, 64, stride=8), :]
        odd = turned[pl.ds(2 * pair + 1, 64, stride=8), :]
        first = jnp.where(low, even, pltpu.roll(odd, 64, 1))
        second = jnp.where(low, pltpu.roll(even, 64, 1), odd)
        for b, rows in enumerate((first, second)):
            rows = rows.reshape(4, 2, 8, 128)
            a, c = rows[:, 0], rows[:, 1]
            near = jnp.where(upper, a, pltpu.roll(c, 4, 1))
            far = jnp.where(upper, pltpu.roll(a, 4, 1), c)
            for yh, part in enumerate((near, far)):
                part = part.reshape(2, 16, 128).astype(BF)
                for xh in range(2):
                    atoms_ref[pair // 2, yh, xh, b, pair % 2] = part[xh]
                send_ref[pair // 2, yh, b, pair % 2] = jnp.where(h == 0, part[1], part[0])


def widen_kernel(weight_ref, out_ref, *, outs):
    zero = jnp.zeros((outs, 64), F32)
    for tx in range(3):
        for ty in range(3):
            w = [weight_ref[9 * tx + 3 * ty + tz].astype(F32) for tz in range(3)]
            for pair, blocks in enumerate(
                (((w[0], w[1]), (zero, w[0])), ((w[2], zero), (w[1], w[2])))
            ):
                wide = jnp.concatenate([jnp.concatenate(two, axis=1) for two in blocks], axis=0)
                row = tx * 256 + pair * 128
                out_ref[row : row + 128, ty * 2 * outs : (ty + 1) * 2 * outs] = wide.T.astype(BF)


def leaf_conv(source, b, k, length, weight_ref):
    parts = [
        source[b, k + dk, dx : dx + length].reshape(length * 16, 128)
        for dx in range(3)
        for dk in range(2)
    ]
    wide = dot(jnp.concatenate(parts, axis=1), weight_ref[...])
    return (
        wide[:, 128:256]
        + pltpu.roll(wide[:, :128], 1, 0)
        + pltpu.roll(wide[:, 256:], length * 16 - 1, 0)
    )


def main_kernel(
    atom_ref, present_ref, own, below_y, above_y, below_z, above_z, w1, w2, w3,
    skip_ref, coarse_ref,
    table, wide, first, second, masks, rows_a, middle_in, rows_b, turned, sems,
):
    copies = [
        pltpu.make_async_copy(
            own.at[zh, yh], table.at[pl.ds((zh * 4 + yh) * 6, 6)], sems.at[zh * 2 + yh]
        )
        for zh in range(2)
        for yh in range(2)
    ]
    for n, source in enumerate((below_y, above_y)):
        copies += [
            pltpu.make_async_copy(
                source.at[zh], table.at[pl.ds((zh * 4 + 2 + n) * 6, 6)], sems.at[4 + n * 2 + zh]
            )
            for zh in range(2)
        ]
    for n, source in enumerate((below_z, above_z)):
        copies.append(
            pltpu.make_async_copy(source, table.at[pl.ds(48 + n * 24, 24)], sems.at[8 + n])
        )
    for copy in copies:
        copy.start()
    table[ABSENT] = jnp.zeros(ATOM, BF)

    low = halves(128)
    y_row = lax.broadcasted_iota(jnp.int32, (16, 128), 0)
    for b in range(2):
        for dx in range(3):
            of_z = []
            for dz in range(3):
                p = [
                    present_ref[b * 27 + 9 * dx + 3 * dy + dz].astype(F32) for dy in range(3)
                ]
                of_z.append(jnp.where(y_row < 4, p[0], jnp.where(y_row < 12, p[1], p[2])))
            masks[b, 0, dx] = of_z[0]
            masks[b, 1, dx] = jnp.where(low, of_z[0], of_z[1])
            masks[b, 2, dx] = of_z[1]
            masks[b, 3, dx] = jnp.where(low, of_z[1], of_z[2])
            masks[b, 4, dx] = of_z[2]

    for copy in copies:
        copy.wait()

    upper = lax.broadcasted_iota(jnp.int32, (1, 1, 8, 1), 2) < 4
    for b in range(2):
        for z in range(4):
            for x in range(4):
                base = ((b * 4 + z) * 4 + x) * 4
                a = [
                    table[atom_ref[base + y]].astype(F32).reshape(2, 2, 8, 128) for y in range(4)
                ]
                r = [pltpu.roll(v.reshape(4, 8, 128), 4, 1).reshape(2, 2, 8, 128) for v in a]
                even = jnp.concatenate(
                    [jnp.where(upper, a[0], r[1]), jnp.where(upper, a[2], r[3])], axis=2
                ).astype(BF)
                odd = jnp.concatenate(
                    [jnp.where(upper, r[0], a[1]), jnp.where(upper, r[2], a[3])], axis=2
                ).astype(BF)
                for pair in range(2):
                    for k in range(2):
                        wide[b, 2 * z + pair, 4 * x + 2 * k] = even[pair, k]
                        wide[b, 2 * z + pair, 4 * x + 2 * k + 1] = odd[pair, k]

    def masked(value, b, pattern, edge):
        mask = [masks[b, pattern, dx][None] for dx in range(3)]
        value = value.reshape(8 + 2 * edge, 16, 128)
        return jnp.concatenate(
            [value[:edge] * mask[0], value[edge : edge + 8] * mask[1], value[edge + 8 :] * mask[2]],
            axis=0,
        )

    for b in range(2):

        def first_step(k, _, b=b):
            value = gelu(leaf_conv(wide, b, k, 14, w1))
            pattern = jnp.minimum(k, 2) + jnp.maximum(k - 4, 0)
            first[b, k] = masked(value, b, pattern, 3).astype(BF)
            return 0

        lax.fori_loop(0, 7, first_step, 0)

    for b in range(2):

        def second_step(k, _, b=b):
            value = gelu(leaf_conv(first, b, k, 12, w2))
            pattern = 2 * (jnp.minimum(k, 1) + jnp.maximum(k - 4, 0))
            second[b, k] = masked(value, b, pattern, 2).astype(BF)
            return 0

        lax.fori_loop(0, 6, second_step, 0)

    for b in range(2):
        layers = []
        for k in range(6):
            v = second[b, k].astype(F32)
            v = (v.reshape(6, 2, 16, 128)[:, 0] + v.reshape(6, 2, 16, 128)[:, 1]).reshape(96, 128)
            v = v + pltpu.roll(v, 64, 1)
            rows_a[b, k] = v + pltpu.roll(v, 95, 0)
            layers.append((rows_a[b, k, pl.ds(0, 48, stride=2), :] * 0.125).astype(BF).astype(F32))
        for pair in range(3):
            middle_in[b, pair] = jnp.where(low, layers[2 * pair], layers[2 * pair + 1])

    operands = []
    for b in range(2):
        for k in range(2):
            operands.append(
                jnp.concatenate(
                    [
                        middle_in[b, k + dk, dx * 8 : dx * 8 + 32]
                        for dx in range(3)
                        for dk in range(2)
                    ],
                    axis=1,
                )
            )
    deep = dot(jnp.concatenate(operands, axis=0).astype(BF), w3[...])
    deep = (
        deep[:, 256:512] + pltpu.roll(deep[:, :256], 1, 0) + pltpu.roll(deep[:, 512:], 127, 0)
    )
    deep = gelu(deep).astype(BF).astype(F32)
    deep = (deep[:, :128] + deep[:, 128:]).reshape(8, 2, 8, 128)
    deep = (deep[:, 0] + deep[:, 1]).reshape(64, 128)
    rows_b[...] = deep + pltpu.roll(deep, 63, 0)
    coarse_ref[...] = (
        jnp.concatenate(
            [rows_b[pl.ds(2, 8, stride=8), :], rows_b[pl.ds(4, 8, stride=8), :]], axis=0
        )
        * 0.125
    ).astype(BF)

    for pair in range(4):
        v = [
            second[b, 1 + pair, 2:10].astype(F32)[:, 4:12, :].reshape(64, 128) for b in range(2)
        ]
        turned[pl.ds(2 * pair, 64, stride=8), :] = jnp.where(low, v[0], pltpu.roll(v[1], 64, 1))
        turned[pl.ds(2 * pair + 1, 64, stride=8), :] = jnp.where(
            low, pltpu.roll(v[0], 64, 1), v[1]
        )
    skip_ref[...] = turned[...].T.astype(BF).reshape(2, 64, 512)


def last_kernel(
    live_ref, core_ref, tap_ref, own, below, above, mine, theirs, w_output, skip_ref, out_ref,
    weights, sems,
):
    core = core_ref[0]
    copies = [
        pltpu.make_async_copy(mine, weights.at[core], sems.at[0]),
        pltpu.make_async_copy(theirs, weights.at[1 - core], sems.at[1]),
    ]
    for copy in copies:
        copy.start()
    tiles = jnp.concatenate([r[...].reshape(96, 128) for r in (own, below, above)], axis=0)
    chosen = (tap_ref[...] == lax.broadcasted_iota(jnp.int32, (432, 288), 1)).astype(F32).astype(BF)
    taps = dot(chosen, tiles).astype(BF)
    for copy in copies:
        copy.wait()
    total = jnp.zeros((16, 256), F32)
    for t in range(27):
        total = total + lax.dot_general(
            taps[t * 16 : (t + 1) * 16],
            weights[t // 14, :, t % 14].reshape(256, 128),
            (((1,), (1,)), ((), ())),
            preferred_element_type=F32,
        )
    hidden = gelu(total).astype(BF)
    coarse = dot(hidden, weights[1, :, 13].reshape(256, 128)).astype(BF).astype(F32)
    coarse = coarse.T[:64].astype(BF)
    row = lax.broadcasted_iota(jnp.int32, (16, 512), 0)
    voxel = lax.broadcasted_iota(jnp.int32, (16, 512), 1)
    place = ((voxel >> 5) & 1) * 8 + ((voxel >> 2) & 1) * 2 + ((voxel >> 8) & 1)
    for b in range(2):
        spread = (row == place + b * 4).astype(F32).astype(BF)
        widened = dot(coarse, spread).astype(BF)
        mixed = dot(w_output[...], jnp.concatenate([skip_ref[b], widened], axis=0))
        mixed = jnp.where(b < live_ref[0], mixed, 0.0)
        out_ref[b] = mixed.astype(BF)


def shape(dims, kind=BF):
    return jax.ShapeDtypeStruct(dims, kind)


def widened_weight(weight, outs):
    return pl.pallas_call(
        functools.partial(widen_kernel, outs=outs),
        out_shape=shape((768, 6 * outs)),
        in_specs=[VMEM],
        out_specs=VMEM,
        compiler_params=PARAMS,
    )(weight)


def shards(
    features, live_counts, neighbours, w_first, w_second, w_middle, w_coarse, w_project, w_output
):
    sizes = (lax.axis_size("grp"), lax.axis_size("ch"))
    g, m = lax.axis_index("grp"), lax.axis_index("ch")
    h, j = m // 8, m % 8

    def moved(value, step_h, step_j, step_g):
        return lax.ppermute(value, AXES, pairs_for(step_h, step_j, step_g, sizes))

    atoms, send, mine = pl.pallas_call(
        pack_kernel,
        out_shape=(shape((2, 2, 2, 2) + ATOM), shape((2, 2, 2) + ATOM), shape((14, 16, 128))),
        in_specs=[SMEM, VMEM, VMEM, VMEM],
        out_specs=(VMEM, VMEM, VMEM),
        scratch_shapes=[pltpu.VMEM((512, 128), F32)],
        compiler_params=PARAMS,
    )(jnp.stack([h, g % 2]).astype(jnp.int32), features, w_coarse, w_project)
    def doubled(value, mask):
        return jnp.concatenate([value, swapped(value, mask, 0, sizes)], axis=0)

    mine = doubled(mine[None], 2)
    beside = moved(send, 1, 0, 0)
    own = jnp.concatenate([atoms, beside[:, :, None]], axis=2)
    near, far, mine, w_first, w_second, w_middle = lax.optimization_barrier(
        (own[:, 1], own[:, 0], mine, w_first, w_second, w_middle)
    )
    below_y = moved(near, 0, 1, 0)
    above_y = moved(far, 0, -1, 0)
    mine = doubled(mine, 8)
    whole = [jnp.concatenate([own[z], below_y[z][None], above_y[z][None]], axis=0) for z in (0, 1)]
    whole[0], whole[1], mine = lax.optimization_barrier((whole[0], whole[1], mine))
    below_z = moved(whole[1], 0, 0, 1)
    above_z = moved(whole[0], 0, 0, -1)
    mine = doubled(mine, 1)
    below_z, above_z, mine = lax.optimization_barrier((below_z, above_z, mine))
    mine = doubled(mine, 4)

    atom_table, tap_table, inner = tables()
    entry = neighbours.reshape(54)
    present = entry >= 0
    group = entry // 32 - g
    member = entry % 32 // 2
    slot = entry % 2
    other = member // 8 != h
    tile = member % 8 - j
    base = (
        jnp.where(group == 0, 0, jnp.where(group < 0, 48, 72))
        + jnp.where(tile == 0, 0, jnp.where(tile < 0, 12, 18))
        + jnp.where(other, 4, 0)
        + slot
    )
    kept = jnp.stack(
        [
            jnp.where(present, base, ABSENT),
            jnp.where(present & (group == 0), 24, 0),
            jnp.where(present & (tile == 0), 6, 0),
            jnp.where(present & ~other, 2, 0),
        ]
    )
    atom_rows = jnp.sum(jnp.asarray(atom_table) * kept[:, None, :], axis=(0, 2))
    code = (
        jnp.where(group == 0, 0, jnp.where(group < 0, 6, 12))
        + jnp.where(tile == 0, 0, jnp.where(tile < 0, 2, 4))
        + jnp.where(other, 1, 0)
    ) * 16 + slot * 4
    code = jnp.where(present, code, -4096)
    tap_rows = jnp.sum(jnp.asarray(tap_table) * code[None], axis=1, keepdims=True) + inner

    w1 = widened_weight(w_first, 64)
    w2 = widened_weight(w_second, 64)
    w3 = widened_weight(w_middle, 128)
    skip, coarse = pl.pallas_call(
        main_kernel,
        out_shape=(shape((2, 64, 512)), shape((16, 128))),
        in_specs=[SMEM] * 2 + [ANY] * 5 + [VMEM] * 3,
        out_specs=(VMEM, VMEM),
        scratch_shapes=[
            pltpu.VMEM((97,) + ATOM, BF),
            pltpu.VMEM((2, 8, 16, 16, 128), BF),
            pltpu.VMEM((2, 7, 14, 16, 128), BF),
            pltpu.VMEM((2, 6, 12, 16, 128), BF),
            pltpu.VMEM((2, 5, 3, 16, 128), F32),
            pltpu.VMEM((2, 6, 96, 128), F32),
            pltpu.VMEM((2, 3, 48, 128), F32),
            pltpu.VMEM((64, 128), F32),
            pltpu.VMEM((512, 128), F32),
            pltpu.SemaphoreType.DMA((10,)),
        ],
        compiler_params=PARAMS,
    )(
        atom_rows,
        present.astype(jnp.int32),
        own.reshape((2, 2, 6) + ATOM),
        below_y.reshape((2, 6) + ATOM),
        above_y.reshape((2, 6) + ATOM),
        below_z.reshape((24,) + ATOM),
        above_z.reshape((24,) + ATOM),
        w1,
        w2,
        w3,
    )

    coarse, mine = lax.optimization_barrier((coarse, mine))
    theirs = swapped(mine, 0, 1, sizes)
    both = jnp.stack([coarse, moved(coarse, 1, 0, 0)])
    layer = jnp.concatenate([both, moved(both, 0, 1, 0), moved(both, 0, -1, 0)], axis=0)
    below, above = moved(layer, 0, 0, 1), moved(layer, 0, 0, -1)
    return pl.pallas_call(
        last_kernel,
        out_shape=shape((2, 64, 512)),
        in_specs=[SMEM] * 2 + [VMEM] * 4 + [ANY] * 2 + [VMEM] * 2,
        out_specs=VMEM,
        scratch_shapes=[
            pltpu.VMEM((2, 16, 14, 16, 128), BF),
            pltpu.SemaphoreType.DMA((2,)),
        ],
        compiler_params=PARAMS,
    )(
        live_counts,
        (g % 2)[None].astype(jnp.int32),
        tap_rows,
        layer,
        below,
        above,
        mine,
        theirs,
        w_output,
        skip,
    )


def solution(mesh):
    return jax.shard_map(
        shards,
        mesh=mesh,
        in_specs=(
            P(AXES, None, None),
            P(AXES),
            P(AXES, None),
            P(),
            P(),
            P(),
            P(None, "ch", None),
            P("ch", None),
            P(),
        ),
        out_specs=P(AXES, None, None),
        check_vma=False,
    )
```

```python
import functools

import jax
import jax.numpy as jnp
import numpy as np
from jax import lax
from jax.experimental import pallas as pl
from jax.experimental.pallas import tpu as pltpu
from jax.sharding import PartitionSpec as P

AXES = ("grp", "ch")
BF = jnp.bfloat16
F32 = jnp.float32
VMEM = pl.BlockSpec(memory_space=pltpu.VMEM)
SMEM = pl.BlockSpec(memory_space=pltpu.SMEM)
ANY = pl.BlockSpec(memory_space=pl.ANY)
HBM = pl.BlockSpec(memory_space=pltpu.HBM)


def params(mebibytes):
    return pltpu.CompilerParams(vmem_limit_bytes=mebibytes * 2**20)

ATOM = (2, 16, 128)
ABSENT = 96


OFFSETS = [(x, y, z) for x in (-1, 0, 1) for y in (-1, 0, 1) for z in (-1, 0, 1)]
STEP = (-1, 0, 0, 1)
HALF = (1, 0, 1, 0)


def tap_table():
    chosen = np.zeros((2, 432, 27), np.float32)
    voxel = np.zeros((432, 1), np.float32)
    for t in range(27):
        for r in range(16):
            y, b, z, x = r // 8, r // 4 % 2, r // 2 % 2, r % 2
            x, y, z = x + t // 9, y + t // 3 % 3, z + t % 3
            chosen[b, t * 16 + r, 9 * STEP[x] + 3 * STEP[y] + STEP[z] + 13] = 1
            voxel[t * 16 + r] = HALF[y] * 8 + HALF[z] * 2 + HALF[x]
    return chosen, voxel


def position():
    m = lax.axis_index("ch")
    g = lax.axis_index("grp")
    return g, m >> 3, m & 7, g & 1


def pairs_for(step_h, step_j, step_g, sizes):
    groups, members = sizes
    tiles = members // 2
    found = []
    for g in range(groups):
        for m in range(members):
            h, j = m // tiles, m % tiles
            to = (1 - h if step_h else h) * tiles + (j + step_j) % tiles
            found.append((g * members + m, (g + step_g) % groups * members + to))
    return found


def exchanged(value, axis_masks, group_mask, sizes):
    groups, members = sizes
    pairs = [
        (g * members + m, (g ^ group_mask) * members + (m ^ axis_masks[g % 2]))
        for g in range(groups)
        for m in range(members)
    ]
    return lax.ppermute(value, AXES, pairs)


def after(value, *others):
    return lax.optimization_barrier((value, *others))[0]


def gelu(v):
    return jax.nn.gelu(v, approximate=True)


def halves(axis_size_lanes):
    return lax.broadcasted_iota(jnp.int32, (1, axis_size_lanes), 1) < 64


def dot(a, b):
    return jnp.dot(a, b, preferred_element_type=F32)


def pack_kernel(features_ref, atoms_ref, packet_ref, turned):
    h = position()[1]
    low = halves(128)
    upper = lax.broadcasted_iota(jnp.int32, (1, 8, 1), 1) < 4
    turned[...] = features_ref[...].astype(F32).reshape(128, 512).T
    for pair in range(4):
        even = turned[pl.ds(2 * pair, 64, stride=8), :]
        odd = turned[pl.ds(2 * pair + 1, 64, stride=8), :]
        first = jnp.where(low, even, pltpu.roll(odd, 64, 1))
        second = jnp.where(low, pltpu.roll(even, 64, 1), odd)
        for b, rows in enumerate((first, second)):
            rows = rows.reshape(4, 2, 8, 128)
            a, c = rows[:, 0], rows[:, 1]
            near = jnp.where(upper, a, pltpu.roll(c, 4, 1))
            far = jnp.where(upper, pltpu.roll(a, 4, 1), c)
            for yh, part in enumerate((near, far)):
                part = part.reshape(2, 16, 128).astype(BF)
                for xh in range(2):
                    atoms_ref[pair // 2, yh, xh, b, pair % 2] = part[xh]
                tile = ((pair // 2 * 2 + yh) * 2 + b) * 2 + pair % 2
                packet_ref[tile] = jnp.where(h == 0, part[1], part[0])


def share_kernel(w_coarse_ref, w_project_ref, packet_in, packet_ref):
    core = position()[3]
    packet_ref[0:16] = packet_in[0:16]

    @pl.when(core == 0)
    def _():
        packet_ref[16:30] = w_coarse_ref[0:14]

    @pl.when(core == 1)
    def _():
        packet_ref[16:29] = w_coarse_ref[14:27]
        project = w_project_ref[...].astype(F32)
        packet_ref[29] = jnp.concatenate([project, jnp.zeros_like(project)], axis=1).astype(BF)


def merge_kernel(atoms_ref, packet_ref, got_ref, far_ref, near_ref, share_ref):
    for yh, out in enumerate((far_ref, near_ref)):
        for zh in range(2):
            out[zh, 0:2] = atoms_ref[zh, yh]
            tile = (zh * 2 + yh) * 4
            out[zh, 2] = got_ref[tile : tile + 4].reshape((2,) + ATOM)
    share_ref[0] = packet_ref[16:30]
    share_ref[1] = got_ref[16:30]


def widen_kernel(
    first_hbm, second_hbm, middle_hbm, w1_ref, w2_ref, w3_ref, first_ref, second_ref, middle_ref, sems
):
    copies = [
        pltpu.make_async_copy(a, b, sems.at[n])
        for n, (a, b) in enumerate(
            ((first_hbm, first_ref), (second_hbm, second_ref), (middle_hbm, middle_ref))
        )
    ]
    for copy in copies:
        copy.start()
    zero = jnp.zeros((64, 64), F32)
    for copy, weight_ref, out_ref in zip(copies, (first_ref, second_ref), (w1_ref, w2_ref)):
        copy.wait()
        for tx in range(3):
            for ty in range(3):
                w = [weight_ref[9 * tx + 3 * ty + tz].astype(F32) for tz in range(3)]
                for pair, blocks in enumerate(
                    (((w[0], w[1]), (zero, w[0])), ((w[2], zero), (w[1], w[2])))
                ):
                    wide = jnp.concatenate([jnp.concatenate(p, axis=1) for p in blocks], axis=0)
                    row = tx * 256 + pair * 128
                    out_ref[row : row + 128, ty * 128 : ty * 128 + 128] = wide.T.astype(BF)
    copies[2].wait()
    w3_ref[...] = jnp.zeros_like(w3_ref)
    for tx in range(3):
        for ty in range(3):
            for tz in range(3):
                for zo in range(2):
                    row = tx * 256 + (tz + zo) * 64
                    column = (ty * 2 + zo) * 128
                    w3_ref[row : row + 64, column : column + 128] = middle_ref[
                        9 * tx + 3 * ty + tz
                    ]


def join_kernel(*refs):
    *sources, out = refs
    row = 0
    for source in sources:
        out[row : row + source.shape[0]] = source[...]
        row += source.shape[0]


def joined(*arrays):
    rows = sum(a.shape[0] for a in arrays)
    return pl.pallas_call(
        join_kernel,
        out_shape=shape((rows,) + arrays[0].shape[1:]),
        in_specs=[VMEM] * len(arrays),
        out_specs=VMEM,
        compiler_params=params(8),
    )(*arrays)


def stack_kernel(far, near, below, above, low_ref, high_ref):
    for z, out in enumerate((low_ref, high_ref)):
        for n, source in enumerate((far, near, below, above)):
            out[n] = source[z]


def leaf_conv(source, b, k, n, length, weight_ref):
    rows = n * length * 16
    parts = [
        source[b, k + dk : k + dk + n, dx : dx + length].reshape(rows, 128)
        for dx in range(3)
        for dk in range(2)
    ]
    wide = dot(jnp.concatenate(parts, axis=1), weight_ref[...])
    return (
        wide[:, 128:256]
        + pltpu.roll(wide[:, :128], 1, 0)
        + pltpu.roll(wide[:, 256:], rows - 1, 0)
    )


def main_kernel(
    neighbour_ref, far, near, below_y, above_y, below_z, above_z, w1, w2, w3,
    skip_ref, coarse_ref,
    table, wide, first, second, masks, rows_a, middle_in, rows_b, turned, sems,
):
    copies = []
    for n, source in enumerate((far, near, below_y, above_y)):
        copies += [
            pltpu.make_async_copy(
                source.at[zh], table.at[pl.ds((zh * 4 + n) * 6, 6)], sems.at[n * 2 + zh]
            )
            for zh in range(2)
        ]
    for n, source in enumerate((below_z, above_z)):
        copies.append(
            pltpu.make_async_copy(source, table.at[pl.ds(48 + n * 24, 24)], sems.at[8 + n])
        )
    for copy in copies:
        copy.start()
    table[ABSENT] = jnp.zeros(ATOM, BF)

    g, h, j, _ = position()
    present, atom_rows = {}, {}
    for b in range(2):
        for n, (dx, dy, dz) in enumerate(OFFSETS):
            entry = neighbour_ref[b, n]
            there = entry >= 0
            present[b, dx, dy, dz] = there.astype(F32)
            apart_g = (entry >> 5) - g
            apart_j = ((entry >> 1) & 7) - j
            other = ((entry >> 4) & 1) != h
            of_z = jnp.where(apart_g < 0, 48, 72)
            of_y = jnp.where(apart_j < 0, 12, 18)
            for z in range(4):
                for x in range(4):
                    for y in range(4):
                        if (STEP[x], STEP[y], STEP[z]) == (dx, dy, dz):
                            row = entry & 1
                            row += jnp.where(apart_g == 0, HALF[z] * 24, of_z) if dz else HALF[z] * 24
                            row += jnp.where(apart_j == 0, HALF[y] * 6, of_y) if dy else HALF[y] * 6
                            row += jnp.where(other, 4, HALF[x] * 2) if dx else HALF[x] * 2
                            atom_rows[b, z, x, y] = jnp.where(there, row, ABSENT)

    low = halves(128)
    y_row = lax.broadcasted_iota(jnp.int32, (16, 128), 0)
    for b in range(2):
        for dx in range(3):
            of_z = []
            for dz in range(3):
                p = [present[b, dx - 1, dy - 1, dz - 1] for dy in range(3)]
                of_z.append(jnp.where(y_row < 4, p[0], jnp.where(y_row < 12, p[1], p[2])))
            masks[b, 0, dx] = of_z[0]
            masks[b, 1, dx] = jnp.where(low, of_z[0], of_z[1])
            masks[b, 2, dx] = of_z[1]
            masks[b, 3, dx] = jnp.where(low, of_z[1], of_z[2])
            masks[b, 4, dx] = of_z[2]

    for copy in copies:
        copy.wait()

    upper = lax.broadcasted_iota(jnp.int32, (1, 1, 8, 1), 2) < 4
    for b in range(2):
        for z in range(4):
            for x in range(4):
                a = [
                    table[atom_rows[b, z, x, y]].astype(F32).reshape(2, 2, 8, 128) for y in range(4)
                ]
                r = [pltpu.roll(v.reshape(4, 8, 128), 4, 1).reshape(2, 2, 8, 128) for v in a]
                even = jnp.concatenate(
                    [jnp.where(upper, a[0], r[1]), jnp.where(upper, a[2], r[3])], axis=2
                ).astype(BF)
                odd = jnp.concatenate(
                    [jnp.where(upper, r[0], a[1]), jnp.where(upper, r[2], a[3])], axis=2
                ).astype(BF)
                for pair in range(2):
                    for k in range(2):
                        wide[b, 2 * z + pair, 4 * x + 2 * k] = even[pair, k]
                        wide[b, 2 * z + pair, 4 * x + 2 * k + 1] = odd[pair, k]

    def masked(value, b, pattern, edge):
        mask = [masks[b, pattern, dx][None] for dx in range(3)]
        value = value.reshape(8 + 2 * edge, 16, 128)
        return jnp.concatenate(
            [value[:edge] * mask[0], value[edge : edge + 8] * mask[1], value[edge + 8 :] * mask[2]],
            axis=0,
        )

    for b in range(2):
        for k, n in ((0, 2), (2, 2), (4, 2), (6, 1)):
            value = gelu(leaf_conv(wide, b, k, n, 14, w1)).reshape(n, 14 * 16, 128)
            for i in range(n):
                pattern = (0, 1, 2, 2, 2, 3, 4)[k + i]
                first[b, k + i] = masked(value[i], b, pattern, 3).astype(BF)
    for b in range(2):
        for k, n in ((0, 2), (2, 2), (4, 2)):
            value = gelu(leaf_conv(first, b, k, n, 12, w2)).reshape(n, 12 * 16, 128)
            for i in range(n):
                pattern = (0, 2, 2, 2, 2, 4)[k + i]
                second[b, k + i] = masked(value[i], b, pattern, 2).astype(BF)

    for b in range(2):
        layers = []
        for k in range(6):
            v = second[b, k].astype(F32)
            v = (v.reshape(6, 2, 16, 128)[:, 0] + v.reshape(6, 2, 16, 128)[:, 1]).reshape(96, 128)
            v = v + pltpu.roll(v, 64, 1)
            rows_a[b, k] = v + pltpu.roll(v, 95, 0)
            layers.append((rows_a[b, k, pl.ds(0, 48, stride=2), :] * 0.125).astype(BF).astype(F32))
        for pair in range(3):
            middle_in[b, pair] = jnp.where(low, layers[2 * pair], layers[2 * pair + 1])

    operands = []
    for b in range(2):
        for k in range(2):
            operands.append(
                jnp.concatenate(
                    [
                        middle_in[b, k + dk, dx * 8 : dx * 8 + 32]
                        for dx in range(3)
                        for dk in range(2)
                    ],
                    axis=1,
                )
            )
    deep = dot(jnp.concatenate(operands, axis=0).astype(BF), w3[...])
    deep = (
        deep[:, 256:512] + pltpu.roll(deep[:, :256], 1, 0) + pltpu.roll(deep[:, 512:], 127, 0)
    )
    deep = gelu(deep).astype(BF).astype(F32)
    deep = (deep[:, :128] + deep[:, 128:]).reshape(8, 2, 8, 128)
    deep = (deep[:, 0] + deep[:, 1]).reshape(64, 128)
    rows_b[...] = deep + pltpu.roll(deep, 63, 0)
    coarse_ref[...] = (
        jnp.concatenate(
            [rows_b[pl.ds(2, 8, stride=8), :], rows_b[pl.ds(4, 8, stride=8), :]], axis=0
        )
        * 0.125
    ).astype(BF)

    for pair in range(4):
        v = [
            second[b, 1 + pair, 2:10].astype(F32)[:, 4:12, :].reshape(64, 128) for b in range(2)
        ]
        turned[pl.ds(2 * pair, 64, stride=8), :] = jnp.where(low, v[0], pltpu.roll(v[1], 64, 1))
        turned[pl.ds(2 * pair + 1, 64, stride=8), :] = jnp.where(
            low, pltpu.roll(v[0], 64, 1), v[1]
        )
    skip_ref[...] = turned[...].T.astype(BF).reshape(2, 64, 512)


def last_kernel(
    live_ref, neighbour_ref, taps_ref, voxel_ref, own, below, above, mine_a, mine_b, theirs_a, theirs_b,
    w_output, skip_ref, out_ref, coarse_ref,
):
    g, h, j, core = position()
    entry = neighbour_ref[...]
    apart_g = (entry >> 5) - g
    apart_j = ((entry >> 1) & 7) - j
    code = (
        jnp.where(apart_g == 0, 0, jnp.where(apart_g < 0, 6, 12))
        + jnp.where(apart_j == 0, 0, jnp.where(apart_j < 0, 2, 4))
        + jnp.where(((entry >> 4) & 1) == h, 0, 1)
    ) * 16 + (entry & 1) * 4
    code = jnp.where(entry >= 0, code, -4096).astype(F32)
    rows = jnp.sum(taps_ref[0] * code[0:1] + taps_ref[1] * code[1:2], axis=1, keepdims=True)
    rows = (rows + voxel_ref[...]).astype(jnp.int32)
    tiles = jnp.concatenate([r[...].reshape(96, 128) for r in (own, below, above)], axis=0)
    chosen = (rows == lax.broadcasted_iota(jnp.int32, (432, 288), 1)).astype(F32).astype(BF)
    taps = dot(chosen, tiles).astype(BF)

    def weight(parts, t):
        if t < 14:
            chosen = [part[:, t] for part in parts]
        else:
            chosen = [part[k : k + 4, t - 14] for k in (0, 4) for part in parts]
        return jnp.concatenate(chosen, axis=0).reshape(256, 128)

    def deepest(early, late):
        total = jnp.zeros((16, 256), F32)
        for t in range(27):
            total = total + lax.dot_general(
                taps[t * 16 : (t + 1) * 16],
                weight(early if t < 14 else late, t),
                (((1,), (1,)), ((), ())),
                preferred_element_type=F32,
            )
        coarse_ref[...] = dot(gelu(total).astype(BF), weight(late, 27))

    @pl.when(core == 0)
    def _():
        deepest((mine_a, mine_b), (theirs_a, theirs_b))

    @pl.when(core == 1)
    def _():
        deepest((theirs_a, theirs_b), (mine_a, mine_b))

    coarse = coarse_ref[...].astype(BF).astype(F32).T[:64].astype(BF)
    row = lax.broadcasted_iota(jnp.int32, (16, 512), 0)
    voxel = lax.broadcasted_iota(jnp.int32, (16, 512), 1)
    place = ((voxel >> 5) & 1) * 8 + ((voxel >> 2) & 1) * 2 + ((voxel >> 8) & 1)
    for b in range(2):
        spread = (row == place + b * 4).astype(F32).astype(BF)
        widened = dot(coarse, spread).astype(BF)
        mixed = dot(w_output[...], jnp.concatenate([skip_ref[b], widened], axis=0))
        mixed = jnp.where(b < live_ref[0], mixed, 0.0)
        out_ref[b] = mixed.astype(BF)


def shape(dims, kind=BF):
    return jax.ShapeDtypeStruct(dims, kind)


def shards(
    features, live_counts, neighbours, w_first, w_second, w_middle, w_coarse, w_project, w_output
):
    sizes = (lax.axis_size("grp"), lax.axis_size("ch"))

    def moved(value, step_h, step_j, step_g):
        return lax.ppermute(value, AXES, pairs_for(step_h, step_j, step_g, sizes))

    atoms, packet = pl.pallas_call(
        pack_kernel,
        out_shape=(shape((2, 2, 2, 2) + ATOM), shape((16, 16, 128))),
        in_specs=[VMEM],
        out_specs=(VMEM, VMEM),
        scratch_shapes=[pltpu.VMEM((512, 128), F32)],
        compiler_params=params(8),
    )(features)
    packet = pl.pallas_call(
        share_kernel,
        out_shape=shape((30, 16, 128)),
        in_specs=[VMEM, VMEM, VMEM],
        out_specs=VMEM,
        compiler_params=params(8),
    )(w_coarse, w_project, packet)
    half_block = shape((2, 3, 2) + ATOM)
    far, near, share = pl.pallas_call(
        merge_kernel,
        out_shape=(half_block, half_block, shape((2, 14, 16, 128))),
        in_specs=[VMEM] * 3,
        out_specs=(VMEM,) * 3,
        compiler_params=params(8),
    )(atoms, packet, moved(packet, 1, 0, 0))
    below_y = moved(near, 0, 1, 0)
    above_y = moved(far, 0, -1, 0)
    share_more = exchanged(share, (2, 2), 0, sizes)
    w1, w2, w3 = pl.pallas_call(
        widen_kernel,
        out_shape=(shape((768, 384)), shape((768, 384)), shape((768, 768))),
        in_specs=[HBM] * 3,
        out_specs=(VMEM,) * 3,
        scratch_shapes=[
            pltpu.VMEM((27, 64, 64), BF),
            pltpu.VMEM((27, 64, 64), BF),
            pltpu.VMEM((27, 64, 128), BF),
            pltpu.SemaphoreType.DMA((3,)),
        ],
        compiler_params=params(8),
    )(after(w_first, near), after(w_second, near), after(jnp.swapaxes(w_middle, 1, 2), near))
    low_z, high_z = pl.pallas_call(
        stack_kernel,
        out_shape=(shape((4, 3, 2) + ATOM),) * 2,
        in_specs=[VMEM] * 4,
        out_specs=(VMEM,) * 2,
        compiler_params=params(8),
    )(far, near, after(below_y, w1), above_y)
    below_z = moved(high_z, 0, 0, 1)
    above_z = moved(low_z, 0, 0, -1)
    share = joined(share, after(share_more, low_z))
    share_more = exchanged(share, (1, 4), 0, sizes)
    mine_a = joined(share, after(share_more, below_z, above_z))
    mine_b = exchanged(mine_a, (4, 1), 0, sizes)
    theirs_a = exchanged(mine_a, (0, 0), 1, sizes)

    skip, coarse = pl.pallas_call(
        main_kernel,
        out_shape=(shape((2, 64, 512)), shape((16, 128))),
        in_specs=[SMEM] + [ANY] * 6 + [VMEM] * 3,
        out_specs=(VMEM, VMEM),
        scratch_shapes=[
            pltpu.VMEM((97,) + ATOM, BF),
            pltpu.VMEM((2, 8, 16, 16, 128), BF),
            pltpu.VMEM((2, 7, 14, 16, 128), BF),
            pltpu.VMEM((2, 6, 12, 16, 128), BF),
            pltpu.VMEM((2, 5, 3, 16, 128), F32),
            pltpu.VMEM((2, 6, 96, 128), F32),
            pltpu.VMEM((2, 3, 48, 128), F32),
            pltpu.VMEM((64, 128), F32),
            pltpu.VMEM((512, 128), F32),
            pltpu.SemaphoreType.DMA((10,)),
        ],
        compiler_params=params(20),
    )(
        after(neighbours, mine_a),
        far.reshape((2, 6) + ATOM),
        near.reshape((2, 6) + ATOM),
        below_y.reshape((2, 6) + ATOM),
        above_y.reshape((2, 6) + ATOM),
        below_z.reshape((24,) + ATOM),
        above_z.reshape((24,) + ATOM),
        w1,
        w2,
        w3,
    )

    theirs_b = exchanged(after(mine_b, coarse), (0, 0), 1, sizes)
    both = joined(coarse[None], moved(coarse, 1, 0, 0)[None])
    layer = joined(both, moved(both, 0, 1, 0), moved(both, 0, -1, 0))
    below, above = moved(layer, 0, 0, 1), moved(layer, 0, 0, -1)
    return pl.pallas_call(
        last_kernel,
        out_shape=shape((2, 64, 512)),
        in_specs=[SMEM] + [VMEM] * 12,
        out_specs=VMEM,
        scratch_shapes=[
            pltpu.VMEM((16, 128), F32),
        ],
        compiler_params=params(8),
    )(
        live_counts,
        neighbours,
        *(jnp.asarray(a) for a in tap_table()),
        layer,
        below,
        above,
        mine_a,
        mine_b,
        theirs_a,
        theirs_b,
        w_output,
        skip,
    )


def solution(mesh):
    return jax.shard_map(
        shards,
        mesh=mesh,
        in_specs=(
            P(AXES, None, None),
            P(AXES),
            P(AXES, None),
            P(),
            P(),
            P(),
            P(None, "ch", None),
            P("ch", None),
            P(),
        ),
        out_specs=P(AXES, None, None),
        check_vma=False,
    )
```

```python
import functools

import jax
import jax.numpy as jnp
import numpy as np
from jax import lax
from jax.experimental import pallas as pl
from jax.experimental.pallas import tpu as pltpu
from jax.sharding import PartitionSpec as P

AXES = ("grp", "ch")
BF = jnp.bfloat16
F32 = jnp.float32
VMEM = pl.BlockSpec(memory_space=pltpu.VMEM)
SMEM = pl.BlockSpec(memory_space=pltpu.SMEM)
ANY = pl.BlockSpec(memory_space=pl.ANY)
HBM = pl.BlockSpec(memory_space=pltpu.HBM)


def params(mebibytes):
    return pltpu.CompilerParams(vmem_limit_bytes=mebibytes * 2**20)


def cost(microseconds):
    return pl.CostEstimate(flops=int(microseconds * 1.15e9), bytes_accessed=0, transcendentals=0)

ATOM = (2, 16, 128)
ABSENT = 96


OFFSETS = [(x, y, z) for x in (-1, 0, 1) for y in (-1, 0, 1) for z in (-1, 0, 1)]
STEP = (-1, 0, 0, 1)
HALF = (1, 0, 1, 0)


def tap_table():
    chosen = np.zeros((2, 432, 27), np.float32)
    voxel = np.zeros((432, 1), np.float32)
    for t in range(27):
        for r in range(16):
            y, b, z, x = r // 8, r // 4 % 2, r // 2 % 2, r % 2
            x, y, z = x + t // 9, y + t // 3 % 3, z + t % 3
            chosen[b, t * 16 + r, 9 * STEP[x] + 3 * STEP[y] + STEP[z] + 13] = 1
            voxel[t * 16 + r] = HALF[y] * 8 + HALF[z] * 2 + HALF[x]
    return chosen, voxel


def position():
    m = lax.axis_index("ch")
    g = lax.axis_index("grp")
    return g, m >> 3, m & 7, g & 1


def permuted(value, along_g, along_h, along_j, sizes):
    groups, members = sizes
    tiles = members // 2
    pairs = []
    for g in range(groups):
        for m in range(members):
            to = along_h(m // tiles) * tiles + along_j(m % tiles, tiles)
            pairs.append((g * members + m, along_g(g, groups) * members + to))
    return lax.ppermute(value, AXES, pairs)


def stay(i, n=0):
    return i


def flip(i, n=0):
    return i ^ 1


def flop(i, n):
    return (((i + 1) ^ 1) - 1) % n


def after(value, *others):
    return lax.optimization_barrier((value, *others))[0]


def gelu(v):
    return jax.nn.gelu(v, approximate=True)


def halves(axis_size_lanes):
    return lax.broadcasted_iota(jnp.int32, (1, axis_size_lanes), 1) < 64


def dot(a, b):
    return jnp.dot(a, b, preferred_element_type=F32)


def started(sources, targets, sems):
    copies = [
        pltpu.make_async_copy(source, target, sems.at[n])
        for n, (source, target) in enumerate(zip(sources, targets))
    ]
    for copy in copies:
        copy.start()
    return copies


def in_hbm(value):
    return pltpu.with_memory_space_constraint(value, pltpu.HBM)


def pack_kernel(
    features_hbm, w_coarse_hbm, w_project_hbm, atoms_ref, packet_ref,
    features_ref, w_coarse_ref, w_project_ref, turned, sems,
):
    copies = started(
        (features_hbm, w_coarse_hbm, w_project_hbm),
        (features_ref, w_coarse_ref, w_project_ref),
        sems,
    )
    copies[0].wait()
    h = position()[1]
    low = halves(128)
    upper = lax.broadcasted_iota(jnp.int32, (1, 8, 1), 1) < 4
    turned[...] = features_ref[...].astype(F32).reshape(128, 512).T
    for pair in range(4):
        even = turned[pl.ds(2 * pair, 64, stride=8), :]
        odd = turned[pl.ds(2 * pair + 1, 64, stride=8), :]
        first = jnp.where(low, even, pltpu.roll(odd, 64, 1))
        second = jnp.where(low, pltpu.roll(even, 64, 1), odd)
        for b, rows in enumerate((first, second)):
            rows = rows.reshape(4, 2, 8, 128)
            a, c = rows[:, 0], rows[:, 1]
            near = jnp.where(upper, a, pltpu.roll(c, 4, 1))
            far = jnp.where(upper, pltpu.roll(a, 4, 1), c)
            for yh, part in enumerate((near, far)):
                part = part.reshape(2, 16, 128).astype(BF)
                for xh in range(2):
                    atoms_ref[pair // 2, yh, xh, b, pair % 2] = part[xh]
                tile = ((pair // 2 * 2 + yh) * 2 + b) * 2 + pair % 2
                packet_ref[tile] = jnp.where(h == 0, part[1], part[0])


    for copy in copies[1:]:
        copy.wait()
    core = position()[3]

    @pl.when(core == 0)
    def _():
        packet_ref[16:30] = w_coarse_ref[0:14]

    @pl.when(core == 1)
    def _():
        packet_ref[16:29] = w_coarse_ref[14:27]
        project = w_project_ref[...].astype(F32)
        packet_ref[29] = jnp.concatenate([project, jnp.zeros_like(project)], axis=1).astype(BF)


def merge_kernel(atoms_ref, packet_ref, got_ref, flip_ref, flop_ref):
    j = position()[2]
    upper = 1 - (j & 1)
    for yh, out in ((upper, flip_ref), (1 - upper, flop_ref)):
        for zh in range(2):
            out[zh * 12 : zh * 12 + 8] = atoms_ref[zh, yh].reshape(8, 16, 128)
            out[zh * 12 + 8 : zh * 12 + 12] = got_ref[pl.ds((zh * 2 + yh) * 4, 4)]
        out[24:38] = packet_ref[16:30]
        out[38:52] = got_ref[16:30]


def widen_kernel(
    first_hbm, second_hbm, middle_hbm, _, w1_ref, w2_ref, w3_ref, first_ref, second_ref, middle_ref, sems
):
    copies = started(
        (first_hbm, second_hbm, middle_hbm), (first_ref, second_ref, middle_ref), sems
    )
    for copy in copies:
        copy.wait()
    zero = jnp.zeros((64, 64), F32)
    for weight_ref, out_ref in ((first_ref, w1_ref), (second_ref, w2_ref)):
        for tx in range(3):
            for ty in range(3):
                w = [weight_ref[9 * tx + 3 * ty + tz].astype(F32) for tz in range(3)]
                for pair, blocks in enumerate(
                    (((w[0], w[1]), (zero, w[0])), ((w[2], zero), (w[1], w[2])))
                ):
                    wide = jnp.concatenate([jnp.concatenate(p, axis=1) for p in blocks], axis=0)
                    row = tx * 256 + pair * 128
                    out_ref[row : row + 128, ty * 128 : ty * 128 + 128] = wide.T.astype(BF)
    w3_ref[...] = jnp.zeros_like(w3_ref)
    for tx in range(3):
        for ty in range(3):
            for tz in range(3):
                for zo in range(2):
                    row = tx * 256 + (tz + zo) * 64
                    column = (ty * 2 + zo) * 128
                    w3_ref[row : row + 64, column : column + 128] = middle_ref[
                        9 * tx + 3 * ty + tz
                    ]


def join_kernel(*refs):
    *sources, out = refs
    row = 0
    for source in sources:
        out[row : row + source.shape[0]] = source[...]
        row += source.shape[0]


def joined(*arrays):
    rows = sum(a.shape[0] for a in arrays)
    return pl.pallas_call(
        join_kernel,
        out_shape=shape((rows,) + arrays[0].shape[1:]),
        in_specs=[VMEM] * len(arrays),
        out_specs=VMEM,
        cost_estimate=cost(0.05),
        compiler_params=params(8),
    )(*arrays)


def stack_kernel(own_flip, own_flop, got_flip, got_flop, flip_ref, flop_ref):
    core = position()[3]
    for zh, out in ((1 - core, flip_ref), (core, flop_ref)):
        for n, source in enumerate((own_flip, own_flop, got_flip, got_flop)):
            out[n * 12 : n * 12 + 12] = source[pl.ds(zh * 12, 12)]


def gather_kernel(own_ref, got_flip, got_flop, three_ref, two_ref):
    j = position()[2]
    three_ref[0:28] = got_flip[24:52]
    three_ref[28:56] = own_ref[24:52]
    three_ref[56:84] = got_flop[24:52]
    two_ref[28:56] = own_ref[24:52]

    @pl.when((j & 1) == 1)
    def _():
        two_ref[0:28] = got_flip[24:52]

    @pl.when((j & 1) == 0)
    def _():
        two_ref[0:28] = got_flop[24:52]


def leaf_conv(source, b, k, n, length, weight_ref):
    rows = n * length * 16
    parts = [
        source[b, k + dk : k + dk + n, dx : dx + length].reshape(rows, 128)
        for dx in range(3)
        for dk in range(2)
    ]
    wide = dot(jnp.concatenate(parts, axis=1), weight_ref[...])
    return (
        wide[:, 128:256]
        + pltpu.roll(wide[:, :128], 1, 0)
        + pltpu.roll(wide[:, 256:], rows - 1, 0)
    )


def atom_rows(neighbour_ref, z_halves):
    g, h, j, _ = position()
    rows = {}
    for b in range(2):
        for n, (dx, dy, dz) in enumerate(OFFSETS):
            if dz not in [STEP[z] for z in z_halves]:
                continue
            entry = neighbour_ref[b, n]
            apart_g = (entry >> 5) ^ g
            apart_j = ((entry >> 1) & 7) ^ j
            other = ((entry >> 4) & 1) != h
            of_z = jnp.where(apart_g == 1, 48, 72)
            of_y = jnp.where(apart_j == 1, 12, 18)
            own_y = ((1 - (j & 1)) * 6, (j & 1) * 6)
            for z in z_halves:
                for x in range(4):
                    for y in range(4):
                        if (STEP[x], STEP[y], STEP[z]) == (dx, dy, dz):
                            row = entry & 1
                            row += jnp.where(apart_g == 0, HALF[z] * 24, of_z) if dz else HALF[z] * 24
                            row += jnp.where(apart_j == 0, own_y[HALF[y]], of_y) if dy else own_y[HALF[y]]
                            row += jnp.where(other, 4, HALF[x] * 2) if dx else HALF[x] * 2
                            rows[b, z, x, y] = jnp.where(entry >= 0, row, ABSENT)
    return rows


def mask_tile(neighbour_ref, b, dx, dz):
    p = [
        (neighbour_ref[b, 9 * dx + 3 * dy + dz] >= 0).astype(F32) for dy in range(3)
    ]
    y_row = lax.broadcasted_iota(jnp.int32, (16, 128), 0)
    return jnp.where(y_row < 4, p[0], jnp.where(y_row < 12, p[1], p[2]))


def assemble(table, rows, b, z, wide, at, first_pair):
    upper = lax.broadcasted_iota(jnp.int32, (1, 1, 8, 1), 2) < 4
    for x in range(4):
        a = [
            table[pl.ds(rows[b, z, x, y] * 2, 2)].astype(F32).reshape(2, 2, 8, 128)
            for y in range(4)
        ]
        r = [pltpu.roll(v.reshape(4, 8, 128), 4, 1).reshape(2, 2, 8, 128) for v in a]
        even = jnp.concatenate(
            [jnp.where(upper, a[0], r[1]), jnp.where(upper, a[2], r[3])], axis=2
        ).astype(BF)
        odd = jnp.concatenate(
            [jnp.where(upper, r[0], a[1]), jnp.where(upper, r[2], a[3])], axis=2
        ).astype(BF)
        for pair in range(2):
            for k in range(2):
                wide[at, first_pair + pair, 4 * x + 2 * k] = even[pair, k]
                wide[at, first_pair + pair, 4 * x + 2 * k + 1] = odd[pair, k]


def over_x(value, mask, edge):
    value = value.reshape(8 + 2 * edge, 16, 128)
    return jnp.concatenate(
        [
            value[:edge] * mask[0][None],
            value[edge : edge + 8] * mask[1][None],
            value[edge + 8 :] * mask[2][None],
        ],
        axis=0,
    )


def own_copies(facing_flip, facing_flop, table, sems):
    core = position()[3]
    return started(
        (facing_flip, facing_flop),
        (table.at[pl.ds((1 - core) * 48, 48)], table.at[pl.ds(core * 48, 48)]),
        sems,
    )


def early_kernel(neighbour_ref, facing_flip, facing_flop, w1, wide, first, table, sems):
    copies = own_copies(facing_flip, facing_flop, table, sems)
    rows = atom_rows(neighbour_ref, (1, 2))
    table[2 * ABSENT : 2 * ABSENT + 2] = jnp.zeros(ATOM, BF)
    for copy in copies:
        copy.wait()
    for b in range(2):
        for z in (1, 2):
            assemble(table, rows, b, z, wide, b, 2 * z - 2)
    for b in range(2):
        mask = [mask_tile(neighbour_ref, b, dx, 1) for dx in range(3)]
        value = gelu(leaf_conv(wide, b, 0, 3, 14, w1)).reshape(3, 14 * 16, 128)
        for i in range(3):
            first[b, i] = over_x(value[i], mask, 3).astype(BF)


def main_kernel(
    neighbour_ref, facing_flip, facing_flop, beside_flip, beside_flop, wide_mid, first_mid,
    w1, w2, w3,
    skip_ref, coarse_ref,
    table, wide, first, second, masks, rows_a, middle_in, rows_b, turned, sems,
):
    copies = own_copies(facing_flip, facing_flop, table, sems)
    for n, source in enumerate((beside_flip, beside_flop)):
        copies.append(
            pltpu.make_async_copy(source, table.at[pl.ds(96 + n * 48, 48)], sems.at[2 + n])
        )
        copies[-1].start()
    table[2 * ABSENT : 2 * ABSENT + 2] = jnp.zeros(ATOM, BF)
    rows = atom_rows(neighbour_ref, (0, 3))

    low = halves(128)
    for b in range(2):
        for dx in range(3):
            of_z = [mask_tile(neighbour_ref, b, dx, dz) for dz in range(3)]
            masks[b, 0, dx] = of_z[0]
            masks[b, 1, dx] = jnp.where(low, of_z[0], of_z[1])
            masks[b, 2, dx] = of_z[1]
            masks[b, 3, dx] = jnp.where(low, of_z[1], of_z[2])
            masks[b, 4, dx] = of_z[2]
        first[b, 2:5] = first_mid[b]
        wide[2 * b, 2] = wide_mid[b, 0]
        wide[2 * b + 1, 0] = wide_mid[b, 3]

    for copy in copies:
        copy.wait()

    for b in range(2):
        assemble(table, rows, b, 0, wide, 2 * b, 0)
        assemble(table, rows, b, 3, wide, 2 * b + 1, 1)

    def masked(value, b, pattern, edge):
        return over_x(value, [masks[b, pattern, dx] for dx in range(3)], edge)

    for b in range(2):
        for side in range(2):
            value = gelu(leaf_conv(wide, 2 * b + side, 0, 2, 14, w1)).reshape(2, 14 * 16, 128)
            for i in range(2):
                pattern = ((0, 1), (3, 4))[side][i]
                first[b, 5 * side + i] = masked(value[i], b, pattern, 3).astype(BF)
    for b in range(2):
        for k, n in ((0, 2), (2, 2), (4, 2)):
            value = gelu(leaf_conv(first, b, k, n, 12, w2)).reshape(n, 12 * 16, 128)
            for i in range(n):
                pattern = (0, 2, 2, 2, 2, 4)[k + i]
                second[b, k + i] = masked(value[i], b, pattern, 2).astype(BF)

    for b in range(2):
        layers = []
        for k in range(6):
            v = second[b, k].astype(F32)
            v = (v.reshape(6, 2, 16, 128)[:, 0] + v.reshape(6, 2, 16, 128)[:, 1]).reshape(96, 128)
            v = v + pltpu.roll(v, 64, 1)
            rows_a[b, k] = v + pltpu.roll(v, 95, 0)
            layers.append((rows_a[b, k, pl.ds(0, 48, stride=2), :] * 0.125).astype(BF).astype(F32))
        for pair in range(3):
            middle_in[b, pair] = jnp.where(low, layers[2 * pair], layers[2 * pair + 1])

    operands = []
    for b in range(2):
        for k in range(2):
            operands.append(
                jnp.concatenate(
                    [
                        middle_in[b, k + dk, dx * 8 : dx * 8 + 32]
                        for dx in range(3)
                        for dk in range(2)
                    ],
                    axis=1,
                )
            )
    deep = dot(jnp.concatenate(operands, axis=0).astype(BF), w3[...])
    deep = (
        deep[:, 256:512] + pltpu.roll(deep[:, :256], 1, 0) + pltpu.roll(deep[:, 512:], 127, 0)
    )
    deep = gelu(deep).astype(BF).astype(F32)
    deep = (deep[:, :128] + deep[:, 128:]).reshape(8, 2, 8, 128)
    deep = (deep[:, 0] + deep[:, 1]).reshape(64, 128)
    rows_b[...] = deep + pltpu.roll(deep, 63, 0)
    coarse_ref[...] = (
        jnp.concatenate(
            [rows_b[pl.ds(2, 8, stride=8), :], rows_b[pl.ds(4, 8, stride=8), :]], axis=0
        )
        * 0.125
    ).astype(BF)

    for pair in range(4):
        v = [
            second[b, 1 + pair, 2:10].astype(F32)[:, 4:12, :].reshape(64, 128) for b in range(2)
        ]
        turned[pl.ds(2 * pair, 64, stride=8), :] = jnp.where(low, v[0], pltpu.roll(v[1], 64, 1))
        turned[pl.ds(2 * pair + 1, 64, stride=8), :] = jnp.where(
            low, pltpu.roll(v[0], 64, 1), v[1]
        )
    skip_ref[...] = turned[...].T.astype(BF).reshape(2, 64, 512)


def last_kernel(
    live_ref, neighbour_ref, taps_ref, voxel_ref, own, below, above, mine_a, mine_b, mine_c,
    theirs_a, theirs_b, theirs_c, w_output, skip_ref, out_ref, coarse_ref,
):
    g, h, j, core = position()
    entry = neighbour_ref[...]
    apart_g = (entry >> 5) ^ g
    apart_j = ((entry >> 1) & 7) ^ j
    code = (
        jnp.where(apart_g == 0, 0, jnp.where(apart_g == 1, 6, 12))
        + jnp.where(apart_j == 0, 0, jnp.where(apart_j == 1, 2, 4))
        + jnp.where(((entry >> 4) & 1) == h, 0, 1)
    ) * 16 + (entry & 1) * 4
    code = jnp.where(entry >= 0, code, -4096).astype(F32)
    rows = jnp.sum(taps_ref[0] * code[0:1] + taps_ref[1] * code[1:2], axis=1, keepdims=True)
    rows = (rows + voxel_ref[...]).astype(jnp.int32)
    tiles = jnp.concatenate([r[...].reshape(96, 128) for r in (own, below, above)], axis=0)
    chosen = (rows == lax.broadcasted_iota(jnp.int32, (432, 288), 1)).astype(F32).astype(BF)
    taps = dot(chosen, tiles).astype(BF)

    def weight(parts, t):
        chosen = [part[:, t % 14] for part in parts]
        return jnp.concatenate(chosen, axis=0).reshape(256, 128)

    def deepest(early, late):
        total = jnp.zeros((16, 256), F32)
        for t in range(27):
            total = total + lax.dot_general(
                taps[t * 16 : (t + 1) * 16],
                weight(early if t < 14 else late, t),
                (((1,), (1,)), ((), ())),
                preferred_element_type=F32,
            )
        coarse_ref[...] = dot(gelu(total).astype(BF), weight(late, 27))

    @pl.when(core == 0)
    def _():
        deepest((mine_a, mine_b, mine_c), (theirs_a, theirs_b, theirs_c))

    @pl.when(core == 1)
    def _():
        deepest((theirs_a, theirs_b, theirs_c), (mine_a, mine_b, mine_c))

    coarse = coarse_ref[...].astype(BF).astype(F32).T[:64].astype(BF)
    row = lax.broadcasted_iota(jnp.int32, (16, 512), 0)
    voxel = lax.broadcasted_iota(jnp.int32, (16, 512), 1)
    place = ((voxel >> 5) & 1) * 8 + ((voxel >> 2) & 1) * 2 + ((voxel >> 8) & 1)
    for b in range(2):
        spread = (row == place + b * 4).astype(F32).astype(BF)
        widened = dot(coarse, spread).astype(BF)
        mixed = dot(w_output[...], jnp.concatenate([skip_ref[b], widened], axis=0))
        mixed = jnp.where(b < live_ref[0], mixed, 0.0)
        out_ref[b] = mixed.astype(BF)


def shape(dims, kind=BF):
    return jax.ShapeDtypeStruct(dims, kind)


def shards(
    features, live_counts, neighbours, w_first, w_second, w_middle, w_coarse, w_project, w_output
):
    sizes = (lax.axis_size("grp"), lax.axis_size("ch"))

    def to_x(value):
        return permuted(value, stay, flip, stay, sizes)

    def to_y(value, along):
        return permuted(value, stay, stay, along, sizes)

    def to_z(value, along):
        return permuted(value, along, stay, stay, sizes)

    atoms, packet = pl.pallas_call(
        pack_kernel,
        out_shape=(shape((2, 2, 2, 2) + ATOM), shape((30, 16, 128))),
        in_specs=[HBM] * 3,
        out_specs=(VMEM, VMEM),
        scratch_shapes=[
            pltpu.VMEM((2, 64, 512), BF),
            pltpu.VMEM((27, 16, 128), BF),
            pltpu.VMEM((16, 64), BF),
            pltpu.VMEM((512, 128), F32),
            pltpu.SemaphoreType.DMA((3,)),
        ],
        cost_estimate=cost(1),
        compiler_params=params(8),
    )(in_hbm(features), in_hbm(w_coarse), in_hbm(w_project))
    own_flip, own_flop = pl.pallas_call(
        merge_kernel,
        out_shape=(shape((52, 16, 128)),) * 2,
        in_specs=[VMEM] * 3,
        out_specs=(VMEM,) * 2,
        cost_estimate=cost(0.1),
        compiler_params=params(8),
    )(atoms, packet, to_x(packet))
    w1, w2, w3 = pl.pallas_call(
        widen_kernel,
        out_shape=(shape((768, 384)), shape((768, 384)), shape((768, 768))),
        in_specs=[HBM] * 3 + [ANY],
        out_specs=(VMEM,) * 3,
        scratch_shapes=[
            pltpu.VMEM((27, 64, 64), BF),
            pltpu.VMEM((27, 64, 64), BF),
            pltpu.VMEM((27, 64, 128), BF),
            pltpu.SemaphoreType.DMA((3,)),
        ],
        cost_estimate=cost(2.5),
        compiler_params=params(8),
    )(in_hbm(w_first), in_hbm(w_second), in_hbm(jnp.swapaxes(w_middle, 1, 2)), own_flip)
    got_flip, got_flop = to_y(own_flip, flip), to_y(own_flop, flop)
    facing_flip, facing_flop = pl.pallas_call(
        stack_kernel,
        out_shape=(shape((48, 16, 128)),) * 2,
        in_specs=[VMEM] * 4,
        out_specs=(VMEM,) * 2,
        cost_estimate=cost(0.05),
        compiler_params=params(8),
    )(own_flip, own_flop, after(got_flip, w1), got_flop)
    beside_flip, beside_flop = to_z(facing_flip, flip), to_z(facing_flop, flop)
    wide_mid, first_mid = pl.pallas_call(
        early_kernel,
        out_shape=(shape((2, 4, 16, 16, 128)), shape((2, 3, 14, 16, 128))),
        in_specs=[SMEM, ANY, ANY, VMEM],
        out_specs=(VMEM,) * 2,
        scratch_shapes=[pltpu.VMEM((194, 16, 128), BF), pltpu.SemaphoreType.DMA((2,))],
        cost_estimate=cost(2.6),
        compiler_params=params(14),
    )(neighbours, facing_flip, facing_flop, w1)
    three, two = pl.pallas_call(
        gather_kernel,
        out_shape=(shape((84, 16, 128)), shape((56, 16, 128))),
        in_specs=[VMEM] * 3,
        out_specs=(VMEM,) * 2,
        cost_estimate=cost(0.05),
        compiler_params=params(8),
    )(own_flip, after(got_flip, wide_mid), got_flop)
    mine = (
        three,
        to_y(three, lambda j, n: (j + 3) % n),
        to_y(two, lambda j, n: (j - 3) % n),
    )

    skip, coarse = pl.pallas_call(
        main_kernel,
        out_shape=(shape((2, 64, 512)), shape((16, 128))),
        in_specs=[SMEM] + [ANY] * 4 + [VMEM] * 5,
        out_specs=(VMEM, VMEM),
        scratch_shapes=[
            pltpu.VMEM((194, 16, 128), BF),
            pltpu.VMEM((4, 3, 16, 16, 128), BF),
            pltpu.VMEM((2, 7, 14, 16, 128), BF),
            pltpu.VMEM((2, 6, 12, 16, 128), BF),
            pltpu.VMEM((2, 5, 3, 16, 128), F32),
            pltpu.VMEM((2, 6, 96, 128), F32),
            pltpu.VMEM((2, 3, 48, 128), F32),
            pltpu.VMEM((64, 128), F32),
            pltpu.VMEM((512, 128), F32),
            pltpu.SemaphoreType.DMA((4,)),
        ],
        cost_estimate=cost(6),
        compiler_params=params(20),
    )(
        after(neighbours, three),
        facing_flip,
        facing_flop,
        beside_flip,
        beside_flop,
        wide_mid,
        first_mid,
        w1,
        w2,
        w3,
    )

    both = joined(coarse[None], to_x(coarse)[None])
    theirs = [to_z(after(part, both), flip) for part in mine]
    layer = joined(both, to_y(both, flip), to_y(both, flop))
    below, above = to_z(layer, flip), to_z(layer, flop)
    return pl.pallas_call(
        last_kernel,
        out_shape=shape((2, 64, 512)),
        in_specs=[SMEM] + [VMEM] * 14,
        out_specs=VMEM,
        scratch_shapes=[
            pltpu.VMEM((16, 128), F32),
        ],
        cost_estimate=cost(2.4),
        compiler_params=params(8),
    )(
        live_counts,
        neighbours,
        *(jnp.asarray(a) for a in tap_table()),
        layer,
        below,
        above,
        *(part.reshape(-1, 14, 16, 128) for part in (*mine, *theirs)),
        w_output,
        skip,
    )


def solution(mesh):
    return jax.shard_map(
        shards,
        mesh=mesh,
        in_specs=(
            P(AXES, None, None),
            P(AXES),
            P(AXES, None),
            P(),
            P(),
            P(),
            P(None, "ch", None),
            P("ch", None),
            P(),
        ),
        out_specs=P(AXES, None, None),
        check_vma=False,
    )
```

```python
import functools

import jax
import jax.numpy as jnp
import numpy as np
from jax import lax
from jax.experimental import pallas as pl
from jax.experimental.pallas import tpu as pltpu
from jax.sharding import PartitionSpec as P

AXES = ("grp", "ch")
BF = jnp.bfloat16
F32 = jnp.float32
VMEM = pl.BlockSpec(memory_space=pltpu.VMEM)
SMEM = pl.BlockSpec(memory_space=pltpu.SMEM)
ANY = pl.BlockSpec(memory_space=pl.ANY)
HBM = pl.BlockSpec(memory_space=pltpu.HBM)


def params(mebibytes):
    return pltpu.CompilerParams(vmem_limit_bytes=mebibytes * 2**20)


def cost(microseconds):
    return pl.CostEstimate(flops=int(microseconds * 1.15e9), bytes_accessed=0, transcendentals=0)

ATOM = (2, 16, 128)
ABSENT = 96


OFFSETS = [(x, y, z) for x in (-1, 0, 1) for y in (-1, 0, 1) for z in (-1, 0, 1)]
STEP = (-1, 0, 0, 1)
HALF = (1, 0, 1, 0)


def tap_table():
    chosen = np.zeros((2, 432, 27), np.float32)
    voxel = np.zeros((432, 1), np.float32)
    for t in range(27):
        for r in range(16):
            y, b, z, x = r // 8, r // 4 % 2, r // 2 % 2, r % 2
            x, y, z = x + t // 9, y + t // 3 % 3, z + t % 3
            chosen[b, t * 16 + r, 9 * STEP[x] + 3 * STEP[y] + STEP[z] + 13] = 1
            voxel[t * 16 + r] = HALF[y] * 8 + HALF[z] * 2 + HALF[x]
    return chosen, voxel


def position():
    m = lax.axis_index("ch")
    g = lax.axis_index("grp")
    return g, m >> 3, m & 7, g & 1


def permuted(value, along_g, along_h, along_j, sizes):
    groups, members = sizes
    tiles = members // 2
    pairs = []
    for g in range(groups):
        for m in range(members):
            to = along_h(m // tiles) * tiles + along_j(m % tiles, tiles)
            pairs.append((g * members + m, along_g(g, groups) * members + to))
    return lax.ppermute(value, AXES, pairs)


def stay(i, n=0):
    return i


def flip(i, n=0):
    return i ^ 1


def flop(i, n):
    return (((i + 1) ^ 1) - 1) % n


def after(value, *others):
    return lax.optimization_barrier((value, *others))[0]


def gelu(v):
    return jax.nn.gelu(v, approximate=True)


def halves(axis_size_lanes):
    return lax.broadcasted_iota(jnp.int32, (1, axis_size_lanes), 1) < 64


def dot(a, b):
    return jnp.dot(a, b, preferred_element_type=F32)


def started(sources, targets, sems):
    copies = [
        pltpu.make_async_copy(source, target, sems.at[n])
        for n, (source, target) in enumerate(zip(sources, targets))
    ]
    for copy in copies:
        copy.start()
    return copies


def in_hbm(value):
    return pltpu.with_memory_space_constraint(value, pltpu.HBM)


def pack_kernel(
    features_hbm, w_coarse_hbm, w_project_hbm, atoms_ref, packet_ref,
    features_ref, w_coarse_ref, w_project_ref, turned, sems,
):
    copies = started(
        (features_hbm, w_coarse_hbm, w_project_hbm),
        (features_ref, w_coarse_ref, w_project_ref),
        sems,
    )
    copies[0].wait()
    h = position()[1]
    low = halves(128)
    upper = lax.broadcasted_iota(jnp.int32, (1, 8, 1), 1) < 4
    turned[...] = features_ref[...].astype(F32).reshape(128, 512).T
    for pair in range(4):
        even = turned[pl.ds(2 * pair, 64, stride=8), :]
        odd = turned[pl.ds(2 * pair + 1, 64, stride=8), :]
        first = jnp.where(low, even, pltpu.roll(odd, 64, 1))
        second = jnp.where(low, pltpu.roll(even, 64, 1), odd)
        for b, rows in enumerate((first, second)):
            rows = rows.reshape(4, 2, 8, 128)
            a, c = rows[:, 0], rows[:, 1]
            near = jnp.where(upper, a, pltpu.roll(c, 4, 1))
            far = jnp.where(upper, pltpu.roll(a, 4, 1), c)
            for yh, part in enumerate((near, far)):
                part = part.reshape(2, 16, 128).astype(BF)
                for xh in range(2):
                    atoms_ref[pair // 2, yh, xh, b, pair % 2] = part[xh]
                tile = ((pair // 2 * 2 + yh) * 2 + b) * 2 + pair % 2
                packet_ref[tile] = jnp.where(h == 0, part[1], part[0])


    for copy in copies[1:]:
        copy.wait()
    core = position()[3]

    @pl.when(core == 0)
    def _():
        packet_ref[16:30] = w_coarse_ref[0:14]

    @pl.when(core == 1)
    def _():
        packet_ref[16:29] = w_coarse_ref[14:27]
        project = w_project_ref[...].astype(F32)
        packet_ref[29] = jnp.concatenate([project, jnp.zeros_like(project)], axis=1).astype(BF)


def merge_kernel(atoms_ref, packet_ref, got_ref, _, flip_ref, flop_ref, share_ref):
    j = position()[2]
    upper = 1 - (j & 1)
    for yh, out in ((upper, flip_ref), (1 - upper, flop_ref)):
        for zh in range(2):
            out[zh * 12 : zh * 12 + 8] = atoms_ref[zh, yh].reshape(8, 16, 128)
            out[zh * 12 + 8 : zh * 12 + 12] = got_ref[pl.ds((zh * 2 + yh) * 4, 4)]
    share_ref[0:14] = packet_ref[16:30]
    share_ref[14:28] = got_ref[16:30]


def widen_kernel(
    first_hbm, second_hbm, middle_hbm, _, w1_ref, w2_ref, w3_ref, first_ref, second_ref, middle_ref, sems
):
    copies = started(
        (first_hbm, second_hbm, middle_hbm), (first_ref, second_ref, middle_ref), sems
    )
    for copy in copies:
        copy.wait()
    zero = jnp.zeros((64, 64), F32)
    for weight_ref, out_ref in ((first_ref, w1_ref), (second_ref, w2_ref)):
        for tx in range(3):
            for ty in range(3):
                w = [weight_ref[9 * tx + 3 * ty + tz].astype(F32) for tz in range(3)]
                for pair, blocks in enumerate(
                    (((w[0], w[1]), (zero, w[0])), ((w[2], zero), (w[1], w[2])))
                ):
                    wide = jnp.concatenate([jnp.concatenate(p, axis=1) for p in blocks], axis=0)
                    row = tx * 256 + pair * 128
                    out_ref[row : row + 128, ty * 128 : ty * 128 + 128] = wide.T.astype(BF)
    w3_ref[...] = jnp.zeros_like(w3_ref)
    for tx in range(3):
        for ty in range(3):
            for tz in range(3):
                for zo in range(2):
                    row = tx * 256 + (tz + zo) * 64
                    column = (ty * 2 + zo) * 128
                    w3_ref[row : row + 64, column : column + 128] = middle_ref[
                        9 * tx + 3 * ty + tz
                    ]


def join_kernel(*refs):
    *sources, out = refs
    row = 0
    for source in sources:
        out[row : row + source.shape[0]] = source[...]
        row += source.shape[0]


def joined(*arrays):
    rows = sum(a.shape[0] for a in arrays)
    return pl.pallas_call(
        join_kernel,
        out_shape=shape((rows,) + arrays[0].shape[1:]),
        in_specs=[VMEM] * len(arrays),
        out_specs=VMEM,
        cost_estimate=cost(0.05),
        compiler_params=params(8),
    )(*arrays)


def stack_kernel(own_flip, own_flop, got_flip, got_flop, flip_ref, flop_ref):
    core = position()[3]
    for zh, out in ((1 - core, flip_ref), (core, flop_ref)):
        for n, source in enumerate((own_flip, own_flop, got_flip, got_flop)):
            out[n * 12 : n * 12 + 12] = source[pl.ds(zh * 12, 12)]


def gather_kernel(own_ref, got_flip, got_flop, _, three_ref, two_ref):
    j = position()[2]
    three_ref[0:28] = got_flip[...]
    three_ref[28:56] = own_ref[...]
    three_ref[56:84] = got_flop[...]
    two_ref[28:56] = own_ref[...]

    @pl.when((j & 1) == 1)
    def _():
        two_ref[0:28] = got_flip[...]

    @pl.when((j & 1) == 0)
    def _():
        two_ref[0:28] = got_flop[...]


def leaf_conv(source, b, k, n, length, weight_ref):
    rows = n * length * 16
    parts = [
        source[b, k + dk : k + dk + n, dx : dx + length].reshape(rows, 128)
        for dx in range(3)
        for dk in range(2)
    ]
    wide = dot(jnp.concatenate(parts, axis=1), weight_ref[...])
    return (
        wide[:, 128:256]
        + pltpu.roll(wide[:, :128], 1, 0)
        + pltpu.roll(wide[:, 256:], rows - 1, 0)
    )


def atom_rows(neighbour_ref, z_halves):
    g, h, j, _ = position()
    rows = {}
    for b in range(2):
        for n, (dx, dy, dz) in enumerate(OFFSETS):
            if dz not in [STEP[z] for z in z_halves]:
                continue
            entry = neighbour_ref[b, n]
            apart_g = (entry >> 5) ^ g
            apart_j = ((entry >> 1) & 7) ^ j
            other = ((entry >> 4) & 1) != h
            of_z = jnp.where(apart_g == 1, 48, 72)
            of_y = jnp.where(apart_j == 1, 12, 18)
            own_y = ((1 - (j & 1)) * 6, (j & 1) * 6)
            for z in z_halves:
                for x in range(4):
                    for y in range(4):
                        if (STEP[x], STEP[y], STEP[z]) == (dx, dy, dz):
                            row = entry & 1
                            row += jnp.where(apart_g == 0, HALF[z] * 24, of_z) if dz else HALF[z] * 24
                            row += jnp.where(apart_j == 0, own_y[HALF[y]], of_y) if dy else own_y[HALF[y]]
                            row += jnp.where(other, 4, HALF[x] * 2) if dx else HALF[x] * 2
                            rows[b, z, x, y] = jnp.where(entry >= 0, row, ABSENT)
    return rows


def mask_tile(neighbour_ref, b, dx, dz):
    p = [
        (neighbour_ref[b, 9 * dx + 3 * dy + dz] >= 0).astype(F32) for dy in range(3)
    ]
    y_row = lax.broadcasted_iota(jnp.int32, (16, 128), 0)
    return jnp.where(y_row < 4, p[0], jnp.where(y_row < 12, p[1], p[2]))


def assemble(table, rows, b, z, wide, at, first_pair):
    upper = lax.broadcasted_iota(jnp.int32, (1, 1, 8, 1), 2) < 4
    for x in range(4):
        a = [
            table[pl.ds(rows[b, z, x, y] * 2, 2)].astype(F32).reshape(2, 2, 8, 128)
            for y in range(4)
        ]
        r = [pltpu.roll(v.reshape(4, 8, 128), 4, 1).reshape(2, 2, 8, 128) for v in a]
        even = jnp.concatenate(
            [jnp.where(upper, a[0], r[1]), jnp.where(upper, a[2], r[3])], axis=2
        ).astype(BF)
        odd = jnp.concatenate(
            [jnp.where(upper, r[0], a[1]), jnp.where(upper, r[2], a[3])], axis=2
        ).astype(BF)
        for pair in range(2):
            for k in range(2):
                wide[at, first_pair + pair, 4 * x + 2 * k] = even[pair, k]
                wide[at, first_pair + pair, 4 * x + 2 * k + 1] = odd[pair, k]


def over_x(value, mask, edge):
    value = value.reshape(8 + 2 * edge, 16, 128)
    return jnp.concatenate(
        [
            value[:edge] * mask[0][None],
            value[edge : edge + 8] * mask[1][None],
            value[edge + 8 :] * mask[2][None],
        ],
        axis=0,
    )


def own_copies(facing_flip, facing_flop, table, sems):
    core = position()[3]
    return started(
        (facing_flip, facing_flop),
        (table.at[pl.ds((1 - core) * 48, 48)], table.at[pl.ds(core * 48, 48)]),
        sems,
    )


def main_kernel(
    neighbour_ref, facing_flip, facing_flop, beside_flip, beside_flop,
    w1, w2, w3,
    skip_ref, coarse_ref,
    table, wide, first, second, masks, rows_a, middle_in, rows_b, turned, sems,
):
    copies = own_copies(facing_flip, facing_flop, table, sems)
    for n, source in enumerate((beside_flip, beside_flop)):
        copies.append(
            pltpu.make_async_copy(source, table.at[pl.ds(96 + n * 48, 48)], sems.at[2 + n])
        )
        copies[-1].start()
    table[2 * ABSENT : 2 * ABSENT + 2] = jnp.zeros(ATOM, BF)
    rows = atom_rows(neighbour_ref, (0, 1, 2, 3))

    low = halves(128)
    for b in range(2):
        for dx in range(3):
            of_z = [mask_tile(neighbour_ref, b, dx, dz) for dz in range(3)]
            masks[b, 0, dx] = of_z[0]
            masks[b, 1, dx] = jnp.where(low, of_z[0], of_z[1])
            masks[b, 2, dx] = of_z[1]
            masks[b, 3, dx] = jnp.where(low, of_z[1], of_z[2])
            masks[b, 4, dx] = of_z[2]

    for copy in copies:
        copy.wait()

    for b in range(2):
        for z in range(4):
            assemble(table, rows, b, z, wide, b, 2 * z)

    def masked(value, b, pattern, edge):
        return over_x(value, [masks[b, pattern, dx] for dx in range(3)], edge)

    for b in range(2):
        for k, n in ((0, 2), (2, 2), (4, 2), (6, 1)):
            value = gelu(leaf_conv(wide, b, k, n, 14, w1)).reshape(n, 14 * 16, 128)
            for i in range(n):
                pattern = (0, 1, 2, 2, 2, 3, 4)[k + i]
                first[b, k + i] = masked(value[i], b, pattern, 3).astype(BF)
    for b in range(2):
        for k, n in ((0, 2), (2, 2), (4, 2)):
            value = gelu(leaf_conv(first, b, k, n, 12, w2)).reshape(n, 12 * 16, 128)
            for i in range(n):
                pattern = (0, 2, 2, 2, 2, 4)[k + i]
                second[b, k + i] = masked(value[i], b, pattern, 2).astype(BF)

    for b in range(2):
        layers = []
        for k in range(6):
            v = second[b, k].astype(F32)
            v = (v.reshape(6, 2, 16, 128)[:, 0] + v.reshape(6, 2, 16, 128)[:, 1]).reshape(96, 128)
            v = v + pltpu.roll(v, 64, 1)
            rows_a[b, k] = v + pltpu.roll(v, 95, 0)
            layers.append((rows_a[b, k, pl.ds(0, 48, stride=2), :] * 0.125).astype(BF).astype(F32))
        for pair in range(3):
            middle_in[b, pair] = jnp.where(low, layers[2 * pair], layers[2 * pair + 1])

    operands = []
    for b in range(2):
        for k in range(2):
            operands.append(
                jnp.concatenate(
                    [
                        middle_in[b, k + dk, dx * 8 : dx * 8 + 32]
                        for dx in range(3)
                        for dk in range(2)
                    ],
                    axis=1,
                )
            )
    deep = dot(jnp.concatenate(operands, axis=0).astype(BF), w3[...])
    deep = (
        deep[:, 256:512] + pltpu.roll(deep[:, :256], 1, 0) + pltpu.roll(deep[:, 512:], 127, 0)
    )
    deep = gelu(deep).astype(BF).astype(F32)
    deep = (deep[:, :128] + deep[:, 128:]).reshape(8, 2, 8, 128)
    deep = (deep[:, 0] + deep[:, 1]).reshape(64, 128)
    rows_b[...] = deep + pltpu.roll(deep, 63, 0)
    coarse_ref[...] = (
        jnp.concatenate(
            [rows_b[pl.ds(2, 8, stride=8), :], rows_b[pl.ds(4, 8, stride=8), :]], axis=0
        )
        * 0.125
    ).astype(BF)

    for pair in range(4):
        v = [
            second[b, 1 + pair, 2:10].astype(F32)[:, 4:12, :].reshape(64, 128) for b in range(2)
        ]
        turned[pl.ds(2 * pair, 64, stride=8), :] = jnp.where(low, v[0], pltpu.roll(v[1], 64, 1))
        turned[pl.ds(2 * pair + 1, 64, stride=8), :] = jnp.where(
            low, pltpu.roll(v[0], 64, 1), v[1]
        )
    skip_ref[...] = turned[...].T.astype(BF).reshape(2, 64, 512)


def last_kernel(
    live_ref, neighbour_ref, taps_ref, voxel_ref, own, below, above, mine_a, mine_b, mine_c,
    theirs_a, theirs_b, theirs_c, w_output, skip_ref, out_ref, coarse_ref,
):
    g, h, j, core = position()
    entry = neighbour_ref[...]
    apart_g = (entry >> 5) ^ g
    apart_j = ((entry >> 1) & 7) ^ j
    code = (
        jnp.where(apart_g == 0, 0, jnp.where(apart_g == 1, 6, 12))
        + jnp.where(apart_j == 0, 0, jnp.where(apart_j == 1, 2, 4))
        + jnp.where(((entry >> 4) & 1) == h, 0, 1)
    ) * 16 + (entry & 1) * 4
    code = jnp.where(entry >= 0, code, -4096).astype(F32)
    rows = jnp.sum(taps_ref[0] * code[0:1] + taps_ref[1] * code[1:2], axis=1, keepdims=True)
    rows = (rows + voxel_ref[...]).astype(jnp.int32)
    tiles = jnp.concatenate([r[...].reshape(96, 128) for r in (own, below, above)], axis=0)
    chosen = (rows == lax.broadcasted_iota(jnp.int32, (432, 288), 1)).astype(F32).astype(BF)
    taps = dot(chosen, tiles).astype(BF)

    def weight(parts, t):
        chosen = [part[:, t % 14] for part in parts]
        return jnp.concatenate(chosen, axis=0).reshape(256, 128)

    def deepest(early, late):
        total = jnp.zeros((16, 256), F32)
        for t in range(27):
            total = total + lax.dot_general(
                taps[t * 16 : (t + 1) * 16],
                weight(early if t < 14 else late, t),
                (((1,), (1,)), ((), ())),
                preferred_element_type=F32,
            )
        coarse_ref[...] = dot(gelu(total).astype(BF), weight(late, 27))

    @pl.when(core == 0)
    def _():
        deepest((mine_a, mine_b, mine_c), (theirs_a, theirs_b, theirs_c))

    @pl.when(core == 1)
    def _():
        deepest((theirs_a, theirs_b, theirs_c), (mine_a, mine_b, mine_c))

    coarse = coarse_ref[...].astype(BF).astype(F32).T[:64].astype(BF)
    row = lax.broadcasted_iota(jnp.int32, (16, 512), 0)
    voxel = lax.broadcasted_iota(jnp.int32, (16, 512), 1)
    place = ((voxel >> 5) & 1) * 8 + ((voxel >> 2) & 1) * 2 + ((voxel >> 8) & 1)
    for b in range(2):
        spread = (row == place + b * 4).astype(F32).astype(BF)
        widened = dot(coarse, spread).astype(BF)
        mixed = dot(w_output[...], jnp.concatenate([skip_ref[b], widened], axis=0))
        mixed = jnp.where(b < live_ref[0], mixed, 0.0)
        out_ref[b] = mixed.astype(BF)


def shape(dims, kind=BF):
    return jax.ShapeDtypeStruct(dims, kind)


def shards(
    features, live_counts, neighbours, w_first, w_second, w_middle, w_coarse, w_project, w_output
):
    sizes = (lax.axis_size("grp"), lax.axis_size("ch"))

    def to_x(value):
        return permuted(value, stay, flip, stay, sizes)

    def to_y(value, along):
        return permuted(value, stay, stay, along, sizes)

    def to_z(value, along):
        return permuted(value, along, stay, stay, sizes)

    atoms, packet = pl.pallas_call(
        pack_kernel,
        out_shape=(shape((2, 2, 2, 2) + ATOM), shape((30, 16, 128))),
        in_specs=[HBM] * 3,
        out_specs=(VMEM, VMEM),
        scratch_shapes=[
            pltpu.VMEM((2, 64, 512), BF),
            pltpu.VMEM((27, 16, 128), BF),
            pltpu.VMEM((16, 64), BF),
            pltpu.VMEM((512, 128), F32),
            pltpu.SemaphoreType.DMA((3,)),
        ],
        cost_estimate=cost(1),
        compiler_params=params(8),
    )(in_hbm(features), in_hbm(w_coarse), in_hbm(w_project))
    beside = to_x(packet)
    w1, w2, w3 = pl.pallas_call(
        widen_kernel,
        out_shape=(shape((768, 384)), shape((768, 384)), shape((768, 768))),
        in_specs=[HBM] * 3 + [ANY],
        out_specs=(VMEM,) * 3,
        scratch_shapes=[
            pltpu.VMEM((27, 64, 64), BF),
            pltpu.VMEM((27, 64, 64), BF),
            pltpu.VMEM((27, 64, 128), BF),
            pltpu.SemaphoreType.DMA((3,)),
        ],
        cost_estimate=cost(2.5),
        compiler_params=params(8),
    )(in_hbm(w_first), in_hbm(w_second), in_hbm(jnp.swapaxes(w_middle, 1, 2)), packet)
    own_flip, own_flop, share = pl.pallas_call(
        merge_kernel,
        out_shape=(shape((24, 16, 128)),) * 2 + (shape((28, 16, 128)),),
        in_specs=[VMEM] * 3 + [ANY],
        out_specs=(VMEM,) * 3,
        cost_estimate=cost(0.1),
        compiler_params=params(8),
    )(atoms, packet, beside, w1)
    got_flip, got_flop = to_y(own_flip, flip), to_y(own_flop, flop)
    share_flip, share_flop = to_y(share, flip), to_y(share, flop)
    facing_flip, facing_flop = pl.pallas_call(
        stack_kernel,
        out_shape=(shape((48, 16, 128)),) * 2,
        in_specs=[VMEM] * 4,
        out_specs=(VMEM,) * 2,
        cost_estimate=cost(2),
        compiler_params=params(8),
    )(own_flip, own_flop, got_flip, got_flop)
    beside_flip, beside_flop = to_z(facing_flip, flip), to_z(facing_flop, flop)
    three, two = pl.pallas_call(
        gather_kernel,
        out_shape=(shape((84, 16, 128)), shape((56, 16, 128))),
        in_specs=[VMEM] * 3 + [ANY],
        out_specs=(VMEM,) * 2,
        cost_estimate=cost(3),
        compiler_params=params(8),
    )(share, share_flip, share_flop, facing_flop)
    mine = (
        three,
        to_y(three, lambda j, n: (j + 3) % n),
        to_y(two, lambda j, n: (j - 3) % n),
    )

    skip, coarse = pl.pallas_call(
        main_kernel,
        out_shape=(shape((2, 64, 512)), shape((16, 128))),
        in_specs=[SMEM] + [ANY] * 4 + [VMEM] * 3,
        out_specs=(VMEM, VMEM),
        scratch_shapes=[
            pltpu.VMEM((194, 16, 128), BF),
            pltpu.VMEM((2, 8, 16, 16, 128), BF),
            pltpu.VMEM((2, 7, 14, 16, 128), BF),
            pltpu.VMEM((2, 6, 12, 16, 128), BF),
            pltpu.VMEM((2, 5, 3, 16, 128), F32),
            pltpu.VMEM((2, 6, 96, 128), F32),
            pltpu.VMEM((2, 3, 48, 128), F32),
            pltpu.VMEM((64, 128), F32),
            pltpu.VMEM((512, 128), F32),
            pltpu.SemaphoreType.DMA((4,)),
        ],
        cost_estimate=cost(7),
        compiler_params=params(20),
    )(
        after(neighbours, three),
        facing_flip,
        facing_flop,
        beside_flip,
        beside_flop,
        w1,
        w2,
        w3,
    )

    both = joined(coarse[None], to_x(coarse)[None])
    theirs = [to_z(after(part, both), flip) for part in mine]
    layer = joined(both, to_y(both, flip), to_y(both, flop))
    below, above = to_z(layer, flip), to_z(layer, flop)
    return pl.pallas_call(
        last_kernel,
        out_shape=shape((2, 64, 512)),
        in_specs=[SMEM] + [VMEM] * 14,
        out_specs=VMEM,
        scratch_shapes=[
            pltpu.VMEM((16, 128), F32),
        ],
        cost_estimate=cost(2.4),
        compiler_params=params(8),
    )(
        live_counts,
        neighbours,
        *(jnp.asarray(a) for a in tap_table()),
        layer,
        below,
        above,
        *(part.reshape(-1, 14, 16, 128) for part in (*mine, *theirs)),
        w_output,
        skip,
    )


def solution(mesh):
    return jax.shard_map(
        shards,
        mesh=mesh,
        in_specs=(
            P(AXES, None, None),
            P(AXES),
            P(AXES, None),
            P(),
            P(),
            P(),
            P(None, "ch", None),
            P("ch", None),
            P(),
        ),
        out_specs=P(AXES, None, None),
        check_vma=False,
    )
```

```python
import functools

import jax
import jax.numpy as jnp
import numpy as np
from jax import lax
from jax.experimental import pallas as pl
from jax.experimental.pallas import tpu as pltpu
from jax.sharding import PartitionSpec as P

AXES = ("grp", "ch")
BF = jnp.bfloat16
F32 = jnp.float32
VMEM = pl.BlockSpec(memory_space=pltpu.VMEM)
SMEM = pl.BlockSpec(memory_space=pltpu.SMEM)
ANY = pl.BlockSpec(memory_space=pl.ANY)
HBM = pl.BlockSpec(memory_space=pltpu.HBM)


def params(mebibytes):
    return pltpu.CompilerParams(vmem_limit_bytes=mebibytes * 2**20)


def cost(microseconds):
    return pl.CostEstimate(flops=int(microseconds * 1.15e9), bytes_accessed=0, transcendentals=0)

ATOM = (2, 16, 128)
ABSENT = 96


OFFSETS = [(x, y, z) for x in (-1, 0, 1) for y in (-1, 0, 1) for z in (-1, 0, 1)]
STEP = (-1, 0, 0, 1)
HALF = (1, 0, 1, 0)


def tap_table():
    chosen = np.zeros((2, 432, 27), np.float32)
    voxel = np.zeros((432, 1), np.float32)
    for t in range(27):
        for r in range(16):
            y, b, z, x = r // 8, r // 4 % 2, r // 2 % 2, r % 2
            x, y, z = x + t // 9, y + t // 3 % 3, z + t % 3
            chosen[b, t * 16 + r, 9 * STEP[x] + 3 * STEP[y] + STEP[z] + 13] = 1
            voxel[t * 16 + r] = HALF[y] * 8 + HALF[z] * 2 + HALF[x]
    return chosen, voxel


def position():
    m = lax.axis_index("ch")
    g = lax.axis_index("grp")
    return g, m >> 3, m & 7, g & 1


def permuted(value, along_g, along_h, along_j, sizes):
    groups, members = sizes
    tiles = members // 2
    pairs = []
    for g in range(groups):
        for m in range(members):
            to = along_h(m // tiles) * tiles + along_j(m % tiles, tiles)
            pairs.append((g * members + m, along_g(g, groups) * members + to))
    return lax.ppermute(value, AXES, pairs)


def stay(i, n=0):
    return i


def flip(i, n=0):
    return i ^ 1


def flop(i, n):
    return (((i + 1) ^ 1) - 1) % n


def after(value, *others):
    return lax.optimization_barrier((value, *others))[0]


def gelu(v):
    return jax.nn.gelu(v, approximate=True)


def halves(axis_size_lanes):
    return lax.broadcasted_iota(jnp.int32, (1, axis_size_lanes), 1) < 64


def dot(a, b):
    return jnp.dot(a, b, preferred_element_type=F32)


def started(sources, targets, sems):
    copies = [
        pltpu.make_async_copy(source, target, sems.at[n])
        for n, (source, target) in enumerate(zip(sources, targets))
    ]
    for copy in copies:
        copy.start()
    return copies


def in_hbm(value):
    return pltpu.with_memory_space_constraint(value, pltpu.HBM)


def pack_kernel(
    features_hbm, w_coarse_hbm, w_project_hbm, atoms_ref, packet_ref,
    features_ref, w_coarse_ref, w_project_ref, turned, sems,
):
    copies = started(
        (features_hbm, w_coarse_hbm, w_project_hbm),
        (features_ref, w_coarse_ref, w_project_ref),
        sems,
    )
    copies[0].wait()
    h = position()[1]
    low = halves(128)
    upper = lax.broadcasted_iota(jnp.int32, (1, 8, 1), 1) < 4
    turned[...] = features_ref[...].astype(F32).reshape(128, 512).T
    for pair in range(4):
        even = turned[pl.ds(2 * pair, 64, stride=8), :]
        odd = turned[pl.ds(2 * pair + 1, 64, stride=8), :]
        first = jnp.where(low, even, pltpu.roll(odd, 64, 1))
        second = jnp.where(low, pltpu.roll(even, 64, 1), odd)
        for b, rows in enumerate((first, second)):
            rows = rows.reshape(4, 2, 8, 128)
            a, c = rows[:, 0], rows[:, 1]
            near = jnp.where(upper, a, pltpu.roll(c, 4, 1))
            far = jnp.where(upper, pltpu.roll(a, 4, 1), c)
            for yh, part in enumerate((near, far)):
                part = part.reshape(2, 16, 128).astype(BF)
                for xh in range(2):
                    atoms_ref[pair // 2, yh, xh, b, pair % 2] = part[xh]
                tile = ((pair // 2 * 2 + yh) * 2 + b) * 2 + pair % 2
                packet_ref[tile] = jnp.where(h == 0, part[1], part[0])


    for copy in copies[1:]:
        copy.wait()
    core = position()[3]

    @pl.when(core == 0)
    def _():
        packet_ref[16:30] = w_coarse_ref[0:14]

    @pl.when(core == 1)
    def _():
        packet_ref[16:29] = w_coarse_ref[14:27]
        project = w_project_ref[...].astype(F32)
        packet_ref[29] = jnp.concatenate([project, jnp.zeros_like(project)], axis=1).astype(BF)


def merge_kernel(atoms_ref, packet_ref, got_ref, _, flip_ref, flop_ref, share_ref):
    j = position()[2]
    upper = 1 - (j & 1)
    for yh, out in ((upper, flip_ref), (1 - upper, flop_ref)):
        for zh in range(2):
            out[zh * 12 : zh * 12 + 8] = atoms_ref[zh, yh].reshape(8, 16, 128)
            out[zh * 12 + 8 : zh * 12 + 12] = got_ref[pl.ds((zh * 2 + yh) * 4, 4)]
    share_ref[0:14] = packet_ref[16:30]
    share_ref[14:28] = got_ref[16:30]


def widen_kernel(
    first_hbm, second_hbm, middle_hbm, _, w1_ref, w2_ref, w3_ref, first_ref, second_ref, middle_ref, sems
):
    copies = started(
        (first_hbm, second_hbm, middle_hbm), (first_ref, second_ref, middle_ref), sems
    )
    for copy in copies:
        copy.wait()
    zero = jnp.zeros((64, 64), F32)
    for weight_ref, out_ref in ((first_ref, w1_ref), (second_ref, w2_ref)):
        for tx in range(3):
            for ty in range(3):
                w = [weight_ref[9 * tx + 3 * ty + tz].astype(F32) for tz in range(3)]
                for pair, blocks in enumerate(
                    (((w[0], w[1]), (zero, w[0])), ((w[2], zero), (w[1], w[2])))
                ):
                    wide = jnp.concatenate([jnp.concatenate(p, axis=1) for p in blocks], axis=0)
                    row = tx * 256 + pair * 128
                    out_ref[row : row + 128, ty * 128 : ty * 128 + 128] = wide.T.astype(BF)
    w3_ref[...] = jnp.zeros_like(w3_ref)
    for tx in range(3):
        for ty in range(3):
            for tz in range(3):
                for zo in range(2):
                    row = tx * 256 + (tz + zo) * 64
                    column = (ty * 2 + zo) * 128
                    w3_ref[row : row + 64, column : column + 128] = middle_ref[
                        9 * tx + 3 * ty + tz
                    ]


def join_kernel(*refs):
    *sources, out = refs
    row = 0
    for source in sources:
        out[row : row + source.shape[0]] = source[...]
        row += source.shape[0]


def joined(*arrays):
    rows = sum(a.shape[0] for a in arrays)
    return pl.pallas_call(
        join_kernel,
        out_shape=shape((rows,) + arrays[0].shape[1:]),
        in_specs=[VMEM] * len(arrays),
        out_specs=VMEM,
        cost_estimate=cost(0.05),
        compiler_params=params(8),
    )(*arrays)


def stack_kernel(own_flip, own_flop, got_flip, got_flop, flip_ref, flop_ref):
    core = position()[3]
    for zh, out in ((1 - core, flip_ref), (core, flop_ref)):
        for n, source in enumerate((own_flip, own_flop, got_flip, got_flop)):
            out[n * 12 : n * 12 + 12] = source[pl.ds(zh * 12, 12)]


def gather_kernel(own_ref, got_flip, got_flop, _, three_ref, two_ref):
    j = position()[2]
    three_ref[0:28] = got_flip[...]
    three_ref[28:56] = own_ref[...]
    three_ref[56:84] = got_flop[...]
    two_ref[28:56] = own_ref[...]

    @pl.when((j & 1) == 1)
    def _():
        two_ref[0:28] = got_flip[...]

    @pl.when((j & 1) == 0)
    def _():
        two_ref[0:28] = got_flop[...]


def leaf_conv(source, b, k, n, length, weight_ref):
    rows = n * length * 16
    parts = [
        source[b, k + dk : k + dk + n, dx : dx + length].reshape(rows, 128)
        for dx in range(3)
        for dk in range(2)
    ]
    wide = dot(jnp.concatenate(parts, axis=1), weight_ref[...])
    return (
        wide[:, 128:256]
        + pltpu.roll(wide[:, :128], 1, 0)
        + pltpu.roll(wide[:, 256:], rows - 1, 0)
    )


def atom_rows(neighbour_ref, z_halves):
    g, h, j, _ = position()
    rows = {}
    for b in range(2):
        for n, (dx, dy, dz) in enumerate(OFFSETS):
            if dz not in [STEP[z] for z in z_halves]:
                continue
            entry = neighbour_ref[b, n]
            apart_g = (entry >> 5) ^ g
            apart_j = ((entry >> 1) & 7) ^ j
            other = ((entry >> 4) & 1) != h
            of_z = jnp.where(apart_g == 1, 48, 72)
            of_y = jnp.where(apart_j == 1, 12, 18)
            own_y = ((1 - (j & 1)) * 6, (j & 1) * 6)
            for z in z_halves:
                for x in range(4):
                    for y in range(4):
                        if (STEP[x], STEP[y], STEP[z]) == (dx, dy, dz):
                            row = entry & 1
                            row += jnp.where(apart_g == 0, HALF[z] * 24, of_z) if dz else HALF[z] * 24
                            row += jnp.where(apart_j == 0, own_y[HALF[y]], of_y) if dy else own_y[HALF[y]]
                            row += jnp.where(other, 4, HALF[x] * 2) if dx else HALF[x] * 2
                            rows[b, z, x, y] = jnp.where(entry >= 0, row, ABSENT)
    return rows


def mask_tile(neighbour_ref, b, dx, dz):
    p = [
        (neighbour_ref[b, 9 * dx + 3 * dy + dz] >= 0).astype(F32) for dy in range(3)
    ]
    y_row = lax.broadcasted_iota(jnp.int32, (16, 128), 0)
    return jnp.where(y_row < 4, p[0], jnp.where(y_row < 12, p[1], p[2]))


def assemble(table, rows, b, z, wide, at, first_pair):
    upper = lax.broadcasted_iota(jnp.int32, (1, 1, 8, 1), 2) < 4
    for x in range(4):
        a = [
            table[pl.ds(rows[b, z, x, y] * 2, 2)].astype(F32).reshape(2, 2, 8, 128)
            for y in range(4)
        ]
        r = [pltpu.roll(v.reshape(4, 8, 128), 4, 1).reshape(2, 2, 8, 128) for v in a]
        even = jnp.concatenate(
            [jnp.where(upper, a[0], r[1]), jnp.where(upper, a[2], r[3])], axis=2
        ).astype(BF)
        odd = jnp.concatenate(
            [jnp.where(upper, r[0], a[1]), jnp.where(upper, r[2], a[3])], axis=2
        ).astype(BF)
        for pair in range(2):
            for k in range(2):
                wide[at, first_pair + pair, 4 * x + 2 * k] = even[pair, k]
                wide[at, first_pair + pair, 4 * x + 2 * k + 1] = odd[pair, k]


def over_x(value, mask, edge):
    value = value.reshape(8 + 2 * edge, 16, 128)
    return jnp.concatenate(
        [
            value[:edge] * mask[0][None],
            value[edge : edge + 8] * mask[1][None],
            value[edge + 8 :] * mask[2][None],
        ],
        axis=0,
    )


def own_copies(facing_flip, facing_flop, table, sems):
    core = position()[3]
    return started(
        (facing_flip, facing_flop),
        (table.at[pl.ds((1 - core) * 48, 48)], table.at[pl.ds(core * 48, 48)]),
        sems,
    )


def main_kernel(
    neighbour_ref, facing_flip, facing_flop, beside_flip, beside_flop,
    w1, w2, w3,
    skip_ref, coarse_ref,
    table, wide, first, second, masks, rows_a, middle_in, rows_b, turned, sems,
):
    copies = own_copies(facing_flip, facing_flop, table, sems)
    for n, source in enumerate((beside_flip, beside_flop)):
        copies.append(
            pltpu.make_async_copy(source, table.at[pl.ds(96 + n * 48, 48)], sems.at[2 + n])
        )
        copies[-1].start()
    table[2 * ABSENT : 2 * ABSENT + 2] = jnp.zeros(ATOM, BF)
    rows = atom_rows(neighbour_ref, (0, 1, 2, 3))

    low = halves(128)
    for b in range(2):
        for dx in range(3):
            of_z = [mask_tile(neighbour_ref, b, dx, dz) for dz in range(3)]
            masks[b, 0, dx] = of_z[0]
            masks[b, 1, dx] = jnp.where(low, of_z[0], of_z[1])
            masks[b, 2, dx] = of_z[1]
            masks[b, 3, dx] = jnp.where(low, of_z[1], of_z[2])
            masks[b, 4, dx] = of_z[2]

    for copy in copies:
        copy.wait()

    for b in range(2):
        for z in range(4):
            assemble(table, rows, b, z, wide, b, 2 * z)

    def masked(value, b, pattern, edge):
        return over_x(value, [masks[b, pattern, dx] for dx in range(3)], edge)

    for b in range(2):
        for k, n in ((0, 2), (2, 2), (4, 2), (6, 1)):
            value = gelu(leaf_conv(wide, b, k, n, 14, w1)).reshape(n, 14 * 16, 128)
            for i in range(n):
                pattern = (0, 1, 2, 2, 2, 3, 4)[k + i]
                first[b, k + i] = masked(value[i], b, pattern, 3).astype(BF)
    for b in range(2):
        for k, n in ((0, 2), (2, 2), (4, 2)):
            value = gelu(leaf_conv(first, b, k, n, 12, w2)).reshape(n, 12 * 16, 128)
            for i in range(n):
                pattern = (0, 2, 2, 2, 2, 4)[k + i]
                second[b, k + i] = masked(value[i], b, pattern, 2).astype(BF)

    for b in range(2):
        layers = []
        for k in range(6):
            v = second[b, k].astype(F32)
            v = (v.reshape(6, 2, 16, 128)[:, 0] + v.reshape(6, 2, 16, 128)[:, 1]).reshape(96, 128)
            v = v + pltpu.roll(v, 64, 1)
            rows_a[b, k] = v + pltpu.roll(v, 95, 0)
            layers.append((rows_a[b, k, pl.ds(0, 48, stride=2), :] * 0.125).astype(BF).astype(F32))
        for pair in range(3):
            middle_in[b, pair] = jnp.where(low, layers[2 * pair], layers[2 * pair + 1])

    operands = []
    for b in range(2):
        for k in range(2):
            operands.append(
                jnp.concatenate(
                    [
                        middle_in[b, k + dk, dx * 8 : dx * 8 + 32]
                        for dx in range(3)
                        for dk in range(2)
                    ],
                    axis=1,
                )
            )
    deep = dot(jnp.concatenate(operands, axis=0).astype(BF), w3[...])
    deep = (
        deep[:, 256:512] + pltpu.roll(deep[:, :256], 1, 0) + pltpu.roll(deep[:, 512:], 127, 0)
    )
    deep = gelu(deep).astype(BF).astype(F32)
    deep = (deep[:, :128] + deep[:, 128:]).reshape(8, 2, 8, 128)
    deep = (deep[:, 0] + deep[:, 1]).reshape(64, 128)
    rows_b[...] = deep + pltpu.roll(deep, 63, 0)
    coarse_ref[...] = (
        jnp.concatenate(
            [rows_b[pl.ds(2, 8, stride=8), :], rows_b[pl.ds(4, 8, stride=8), :]], axis=0
        )
        * 0.125
    ).astype(BF)

    for pair in range(4):
        v = [
            second[b, 1 + pair, 2:10].astype(F32)[:, 4:12, :].reshape(64, 128) for b in range(2)
        ]
        turned[pl.ds(2 * pair, 64, stride=8), :] = jnp.where(low, v[0], pltpu.roll(v[1], 64, 1))
        turned[pl.ds(2 * pair + 1, 64, stride=8), :] = jnp.where(
            low, pltpu.roll(v[0], 64, 1), v[1]
        )
    skip_ref[...] = turned[...].T.astype(BF).reshape(2, 64, 512)


def choose_kernel(neighbour_ref, taps_ref, voxel_ref, chosen_ref):
    g, h, j, _ = position()
    entry = neighbour_ref[...]
    apart_g = (entry >> 5) ^ g
    apart_j = ((entry >> 1) & 7) ^ j
    code = (
        jnp.where(apart_g == 0, 0, jnp.where(apart_g == 1, 6, 12))
        + jnp.where(apart_j == 0, 0, jnp.where(apart_j == 1, 2, 4))
        + jnp.where(((entry >> 4) & 1) == h, 0, 1)
    ) * 16 + (entry & 1) * 4
    code = jnp.where(entry >= 0, code, -4096).astype(F32)
    rows = jnp.sum(taps_ref[0] * code[0:1] + taps_ref[1] * code[1:2], axis=1, keepdims=True)
    rows = (rows + voxel_ref[...]).astype(jnp.int32)
    chosen_ref[...] = (rows == lax.broadcasted_iota(jnp.int32, (432, 288), 1)).astype(F32).astype(BF)


def last_kernel(
    live_ref, chosen_ref, own, below, above, mine_a, mine_b, mine_c,
    theirs_a, theirs_b, theirs_c, w_output, skip_ref, out_ref, coarse_ref,
):
    core = position()[3]
    tiles = jnp.concatenate([r[...].reshape(96, 128) for r in (own, below, above)], axis=0)
    taps = dot(chosen_ref[...], tiles).astype(BF)

    def weight(parts, t):
        chosen = [part[:, t % 14] for part in parts]
        return jnp.concatenate(chosen, axis=0).reshape(256, 128)

    def deepest(early, late):
        total = jnp.zeros((16, 256), F32)
        for t in range(27):
            total = total + lax.dot_general(
                taps[t * 16 : (t + 1) * 16],
                weight(early if t < 14 else late, t),
                (((1,), (1,)), ((), ())),
                preferred_element_type=F32,
            )
        coarse_ref[...] = dot(gelu(total).astype(BF), weight(late, 27))

    @pl.when(core == 0)
    def _():
        deepest((mine_a, mine_b, mine_c), (theirs_a, theirs_b, theirs_c))

    @pl.when(core == 1)
    def _():
        deepest((theirs_a, theirs_b, theirs_c), (mine_a, mine_b, mine_c))

    coarse = coarse_ref[...].astype(BF).astype(F32).T[:64].astype(BF)
    row = lax.broadcasted_iota(jnp.int32, (16, 512), 0)
    voxel = lax.broadcasted_iota(jnp.int32, (16, 512), 1)
    place = ((voxel >> 5) & 1) * 8 + ((voxel >> 2) & 1) * 2 + ((voxel >> 8) & 1)
    for b in range(2):
        spread = (row == place + b * 4).astype(F32).astype(BF)
        widened = dot(coarse, spread).astype(BF)
        mixed = dot(w_output[...], jnp.concatenate([skip_ref[b], widened], axis=0))
        mixed = jnp.where(b < live_ref[0], mixed, 0.0)
        out_ref[b] = mixed.astype(BF)


def shape(dims, kind=BF):
    return jax.ShapeDtypeStruct(dims, kind)


def shards(
    features, live_counts, neighbours, w_first, w_second, w_middle, w_coarse, w_project, w_output
):
    sizes = (lax.axis_size("grp"), lax.axis_size("ch"))

    def to_x(value):
        return permuted(value, stay, flip, stay, sizes)

    def to_y(value, along):
        return permuted(value, stay, stay, along, sizes)

    def to_z(value, along):
        return permuted(value, along, stay, stay, sizes)

    atoms, packet = pl.pallas_call(
        pack_kernel,
        out_shape=(shape((2, 2, 2, 2) + ATOM), shape((30, 16, 128))),
        in_specs=[HBM] * 3,
        out_specs=(VMEM, VMEM),
        scratch_shapes=[
            pltpu.VMEM((2, 64, 512), BF),
            pltpu.VMEM((27, 16, 128), BF),
            pltpu.VMEM((16, 64), BF),
            pltpu.VMEM((512, 128), F32),
            pltpu.SemaphoreType.DMA((3,)),
        ],
        cost_estimate=cost(1),
        compiler_params=params(8),
    )(in_hbm(features), in_hbm(w_coarse), in_hbm(w_project))
    beside = to_x(packet)
    w1, w2, w3 = pl.pallas_call(
        widen_kernel,
        out_shape=(shape((768, 384)), shape((768, 384)), shape((768, 768))),
        in_specs=[HBM] * 3 + [ANY],
        out_specs=(VMEM,) * 3,
        scratch_shapes=[
            pltpu.VMEM((27, 64, 64), BF),
            pltpu.VMEM((27, 64, 64), BF),
            pltpu.VMEM((27, 64, 128), BF),
            pltpu.SemaphoreType.DMA((3,)),
        ],
        cost_estimate=cost(2.5),
        compiler_params=params(8),
    )(in_hbm(w_first), in_hbm(w_second), in_hbm(jnp.swapaxes(w_middle, 1, 2)), packet)
    own_flip, own_flop, share = pl.pallas_call(
        merge_kernel,
        out_shape=(shape((24, 16, 128)),) * 2 + (shape((28, 16, 128)),),
        in_specs=[VMEM] * 3 + [ANY],
        out_specs=(VMEM,) * 3,
        cost_estimate=cost(0.1),
        compiler_params=params(8),
    )(atoms, packet, beside, w1)
    got_flip, got_flop = to_y(own_flip, flip), to_y(own_flop, flop)
    share_flip, share_flop = to_y(share, flip), to_y(share, flop)
    facing_flip, facing_flop = pl.pallas_call(
        stack_kernel,
        out_shape=(shape((48, 16, 128)),) * 2,
        in_specs=[VMEM] * 4,
        out_specs=(VMEM,) * 2,
        cost_estimate=cost(2),
        compiler_params=params(8),
    )(own_flip, own_flop, got_flip, got_flop)
    beside_flip, beside_flop = to_z(facing_flip, flip), to_z(facing_flop, flop)
    three, two = pl.pallas_call(
        gather_kernel,
        out_shape=(shape((84, 16, 128)), shape((56, 16, 128))),
        in_specs=[VMEM] * 3 + [ANY],
        out_specs=(VMEM,) * 2,
        cost_estimate=cost(3),
        compiler_params=params(8),
    )(share, share_flip, share_flop, facing_flop)
    mine = (
        three,
        to_y(three, lambda j, n: (j + 3) % n),
        to_y(two, lambda j, n: (j - 3) % n),
    )

    skip, coarse = pl.pallas_call(
        main_kernel,
        out_shape=(shape((2, 64, 512)), shape((16, 128))),
        in_specs=[SMEM] + [ANY] * 4 + [VMEM] * 3,
        out_specs=(VMEM, VMEM),
        scratch_shapes=[
            pltpu.VMEM((194, 16, 128), BF),
            pltpu.VMEM((2, 8, 16, 16, 128), BF),
            pltpu.VMEM((2, 7, 14, 16, 128), BF),
            pltpu.VMEM((2, 6, 12, 16, 128), BF),
            pltpu.VMEM((2, 5, 3, 16, 128), F32),
            pltpu.VMEM((2, 6, 96, 128), F32),
            pltpu.VMEM((2, 3, 48, 128), F32),
            pltpu.VMEM((64, 128), F32),
            pltpu.VMEM((512, 128), F32),
            pltpu.SemaphoreType.DMA((4,)),
        ],
        cost_estimate=cost(7),
        compiler_params=params(20),
    )(
        after(neighbours, three),
        facing_flip,
        facing_flop,
        beside_flip,
        beside_flop,
        w1,
        w2,
        w3,
    )

    chosen = pl.pallas_call(
        choose_kernel,
        out_shape=shape((432, 288)),
        in_specs=[VMEM] * 3,
        out_specs=VMEM,
        cost_estimate=cost(0.5),
        compiler_params=params(8),
    )(neighbours, *(jnp.asarray(a) for a in tap_table()))
    both = joined(coarse[None], to_x(coarse)[None])
    theirs = [to_z(after(part, both), flip) for part in mine]
    layer = joined(both, to_y(both, flip), to_y(both, flop))
    below, above = to_z(layer, flip), to_z(layer, flop)
    return pl.pallas_call(
        last_kernel,
        out_shape=shape((2, 64, 512)),
        in_specs=[SMEM] + [VMEM] * 12,
        out_specs=VMEM,
        scratch_shapes=[
            pltpu.VMEM((16, 128), F32),
        ],
        cost_estimate=cost(2.4),
        compiler_params=params(8),
    )(
        live_counts,
        chosen,
        layer,
        below,
        above,
        *(part.reshape(-1, 14, 16, 128) for part in (*mine, *theirs)),
        w_output,
        skip,
    )


def solution(mesh):
    return jax.shard_map(
        shards,
        mesh=mesh,
        in_specs=(
            P(AXES, None, None),
            P(AXES),
            P(AXES, None),
            P(),
            P(),
            P(),
            P(None, "ch", None),
            P("ch", None),
            P(),
        ),
        out_specs=P(AXES, None, None),
        check_vma=False,
    )
```
